256 devices in a mesh: gx: 4 (over x), gy: 2 (over core), gz: 32 (over z, y).
Axes of the slice: x: 4, y: 4, z: 8, core: 2. Of those that a mesh axis runs over, the one named last changes fastest.
Arguments:
- component_mass_shares: float32 [9, 32, 64, 4096], P(None, 'gx', 'gy', 'gz'), may hold values from 0 to 1
- kelvin_values: float32 [32, 64, 4096], P('gx', 'gy', 'gz'), may hold values from 0.8 to 2.5
- reciprocal_pairwise_spreads: float32 [9, 9], replicated, may hold values from 0.5 to 5
- kinetic_coupling_table: float32 [9, 9], replicated, may hold values from 0.05 to 0.5
- burning_first_tiles: int32 [4, 2, 32, 256], P('gx', 'gy', 'gz'), may hold values from 0 to 255, each once within a row
- burning_tile_tally: int32 [4, 64], P('gx'), may hold values from 1 to 64, 1024 in all within a row
Outputs:
- species_out: float32 [9, 32, 64, 4096], P(None, 'gx', 'gy', 'gz')
The draws below stay inside these ranges and needn't reach their ends.
Inputs may be any that keep to these rules, and one draw needn't show every extreme that they name: `burning_first_tiles`: each device's row is a permutation of its 256 blocks; block e is the line of cells at local position (e // 32, e % 32) along the spanwise dimension. `burning_tile_tally`: row a holds the counts of the 64 devices with gx index a, in the order b * (devices along gz) + c; every row sums to 1024.
All inputs are finite; a program needn't handle non-finite values.
Results may differ from the reference program's by a relative error of at most 0.000098.
Values sent between devices are 32-bit elements; how exact they have to be, the bound alone decides.
No kernel may reach another device: no remote copies, remote signals or barrier semaphores. Data moves between devices by JAX's collectives and lax.ppermute only.
A program may use at most 192 MiB of HBM per device.

```python
import math
import jax
import jax.numpy as jnp
import numpy as np
from jax import lax

NS = 9
CX = 8
CY = 32
LOCAL_WIDE_PTS = 128
SLOTS = 64
MEANB = 16
GROUP = 64
DOWNWIND_PTS = 32
TRANSVERSE_PTS = 64
SPANWISE_PTS = 4096
N_GX = 4
N_GY = 2
N_GZ = 32


def block_scale(stream_key, shape, split, least, largest):
    level = 1.0
    for dim, parts in split:
        steps = jax.random.uniform(jax.random.fold_in(jax.random.fold_in(stream_key, 6), dim), (parts,), jnp.float32, least / len(split), largest / len(split))
        level = level * jnp.repeat(jnp.exp(steps), shape[dim] // parts).reshape((-1,) + (1,) * (len(shape) - 1 - dim))
    return level


def length_profile(amount, total, reach, skew):
    weights = [(1 << 20) // math.isqrt(grade ** skew) + 1 for grade in range(2, amount + 1)]
    surplus, given = total - reach - (amount - 1), [1] * (amount - 1)
    while surplus > 0:
        candidates = [i for i in range(amount - 1) if given[i] < reach]
        mass, left = sum([weights[i] for i in candidates]), surplus
        for i in candidates:
            more = min(reach - given[i], max(1, left * weights[i] // mass), surplus)
            given[i] = given[i] + more
            surplus = surplus - more
    return np.array([reach] + given)


def uneven_parts(stream_key, number_of, total, limit, skew):
    if number_of == 2:
        one = jax.random.randint(stream_key, (), max(1, total - limit), min(limit, total - 1) + 1)
        return jnp.stack([one, total - one])
    sizes = jnp.asarray(length_profile(number_of, total, limit, skew), jnp.int32)
    pairs = (number_of - 1) // 2
    donor, sink = sizes[1:1 + 2 * pairs:2], sizes[2:2 + 2 * pairs:2]
    margin = jnp.minimum(donor - 1, limit - sink)
    shifted = jax.random.randint(jax.random.fold_in(stream_key, 1), (pairs,), 0, 1 << 20) % (margin + 1)
    sizes = sizes.at[1:1 + 2 * pairs:2].set(donor - shifted).at[2:2 + 2 * pairs:2].set(sink + shifted)
    return sizes[jax.random.permutation(jax.random.fold_in(stream_key, 2), number_of)]


def setup_inputs(seed: int = 0) -> dict:
    streams_of = jax.random.split(jax.random.key(seed), 7)
    return {
        "component_mass_shares": jnp.clip(1.0 * jax.random.uniform(streams_of[0], (NS, DOWNWIND_PTS, TRANSVERSE_PTS, SPANWISE_PTS), jnp.float32) ** block_scale(streams_of[0], (NS, DOWNWIND_PTS, TRANSVERSE_PTS, SPANWISE_PTS), ((1, 4), (2, 2), (3, 32)), -0.2, 0.2), 0.0, 1.0),
        "kelvin_values": jnp.clip(0.8 + 1.7 * jax.random.uniform(streams_of[1], (DOWNWIND_PTS, TRANSVERSE_PTS, SPANWISE_PTS), jnp.float32) ** block_scale(streams_of[1], (DOWNWIND_PTS, TRANSVERSE_PTS, SPANWISE_PTS), ((0, 4), (1, 2), (2, 32)), -0.2, 0.2), 0.8, 2.5),
        "reciprocal_pairwise_spreads": jnp.clip(jnp.exp(jax.random.uniform(streams_of[2], (NS, NS), jnp.float32, math.log(0.5), math.log(5.0))), 0.5, 5.0),
        "kinetic_coupling_table": jnp.clip(jnp.exp(jax.random.uniform(streams_of[3], (NS, NS), jnp.float32, math.log(0.05), math.log(0.5))), 0.05, 0.5),
        "burning_first_tiles": jax.vmap(lambda own: jax.random.permutation(own, CX * CY))(jax.random.split(streams_of[4], N_GX * N_GY * N_GZ)).reshape((N_GX, N_GY, N_GZ, CX * CY)).astype(jnp.int32),
        "burning_tile_tally": jax.vmap(lambda own: uneven_parts(own, GROUP, GROUP * MEANB, SLOTS, 2))(jax.random.split(streams_of[5], N_GX)).reshape((N_GX, GROUP)).astype(jnp.int32),
    }


coefficients = (0.8, -0.2, 4.0 / 105.0, -1.0 / 280.0)
flow_step = 0.1
chem_step = 0.1
gamma_ros = 1.0 + 0.5 ** 0.5
barrier_height = 2.0

def reacting_advance(molar_shares, local_heat_levels, kinetic_coupling_table):
    species_count = kinetic_coupling_table.shape[0]
    identity = jnp.eye(species_count, dtype=jnp.float32)
    off_diagonal = kinetic_coupling_table * (1.0 - identity)
    consume = 1.25 * lax.optimization_barrier(jnp.sum(off_diagonal, axis=0)) + jnp.diagonal(kinetic_coupling_table)
    reaction = off_diagonal - identity * consume[None, :]
    kinetic_speed = jnp.exp(barrier_height * (1.0 - 1.0 / local_heat_levels))
    scaled = gamma_ros * chem_step * kinetic_speed

    def production(state):
        return kinetic_speed * jnp.tensordot(reaction, state * state, axes=(1, 0), precision=lax.Precision.HIGHEST)
    factors = [[(1.0 if i == j else 0.0) - scaled * (2.0 * reaction[i, j]) * molar_shares[j] for j in range(species_count)] for i in range(species_count)]
    for p in range(species_count):
        for r in range(p + 1, species_count):
            multiplier = factors[r][p] / factors[p][p]
            factors[r][p] = multiplier
            for c in range(p + 1, species_count):
                factors[r][c] = factors[r][c] - multiplier * factors[p][c]

    def substitute(source):
        unknown = [source[i] for i in range(species_count)]
        for r in range(species_count):
            for c in range(r):
                unknown[r] = unknown[r] - factors[r][c] * unknown[c]
        for r in reversed(range(species_count)):
            for c in range(r + 1, species_count):
                unknown[r] = unknown[r] - factors[r][c] * unknown[c]
            unknown[r] = unknown[r] / factors[r][r]
        return jnp.stack(unknown)
    section_one = substitute(production(molar_shares))
    section_two = substitute(production(molar_shares + chem_step * section_one) - 2.0 * section_one)
    return chem_step * (1.5 * section_one + 0.5 * section_two)

def derivative(values, direction):
    summed = None
    for m in range(4):
        contribution = coefficients[m] * (jnp.roll(values, -(m + 1), direction) - jnp.roll(values, m + 1, direction))
        summed = contribution if summed is None else summed + contribution
    return summed

def reference(component_mass_shares, kelvin_values, reciprocal_pairwise_spreads, kinetic_coupling_table, burning_first_tiles, burning_tile_tally):
    heat_levels_grid = kelvin_values * jnp.sqrt(kelvin_values)

    def one_species(species_index):
        weights = lax.dynamic_index_in_dim(reciprocal_pairwise_spreads, species_index, 0, keepdims=False)
        combined_gases = jnp.tensordot(weights, component_mass_shares, axes=(0, 0), precision=lax.Precision.HIGHEST)
        averaging_formula = heat_levels_grid / (1.0 + combined_gases)
        target = lax.dynamic_index_in_dim(component_mass_shares, species_index, 0, keepdims=False)
        result = None
        for direction in range(3):
            addend = derivative(averaging_formula * derivative(target, direction), direction)
            result = addend if result is None else result + addend
        return result
    diffusion = lax.map(one_species, jnp.arange(NS, dtype=jnp.int32))
    pencils = component_mass_shares.reshape(NS, DOWNWIND_PTS, TRANSVERSE_PTS, N_GZ, LOCAL_WIDE_PTS)
    heat_line_strips = kelvin_values.reshape(DOWNWIND_PTS, TRANSVERSE_PTS, N_GZ, LOCAL_WIDE_PTS)
    chosen = burning_first_tiles[..., :SLOTS]
    along_x = (jnp.arange(N_GX, dtype=jnp.int32) * CX)[:, None, None, None] + chosen // CY
    along_y = (jnp.arange(N_GY, dtype=jnp.int32) * CY)[None, :, None, None] + chosen % CY
    along_z = jnp.zeros_like(chosen) + jnp.arange(N_GZ, dtype=jnp.int32)[None, None, :, None]
    counts = burning_tile_tally.reshape(N_GX, N_GY, N_GZ)[..., None]
    active = (jnp.arange(SLOTS, dtype=jnp.int32)[None, None, None, :] < counts).astype(jnp.float32)
    mass_blocks = pencils[:, along_x, along_y, along_z, :]
    heat_blocks = heat_line_strips[along_x, along_y, along_z, :]
    change = reacting_advance(mass_blocks, heat_blocks, kinetic_coupling_table) * active[..., None]
    pencils_change = jnp.zeros_like(pencils).at[:, along_x, along_y, along_z, :].add(change)
    return flow_step * diffusion + pencils_change.reshape(NS, DOWNWIND_PTS, TRANSVERSE_PTS, SPANWISE_PTS)
```

```python
import functools

import jax
import jax.numpy as jnp
import numpy as np
from jax import lax
from jax.experimental import pallas as pl
from jax.experimental.pallas import tpu as pltpu
from jax.sharding import PartitionSpec as P

SLOTS = 64
EDGE = 8

coefficients = (0.8, -0.2, 4.0 / 105.0, -1.0 / 280.0)
flow_step = 0.1
chem_step = 0.1
gamma_ros = 1.0 + 0.5**0.5
barrier_height = 2.0

VMEM = pl.BlockSpec(memory_space=pltpu.VMEM)
SMEM = pl.BlockSpec(memory_space=pltpu.SMEM)
PARAMS = pltpu.CompilerParams(vmem_limit_bytes=24 * 1024 * 1024)


def f32(*shape):
    return jax.ShapeDtypeStruct(shape, jnp.float32)


def stencil(take):
    total = None
    for m in range(1, 5):
        term = coefficients[m - 1] * (take(m) - take(-m))
        total = term if total is None else total + term
    return total


def weighted(table, k, shares):
    total = table[k, 0] * shares[0]
    for j in range(1, len(shares)):
        total = total + table[k, j] * shares[j]
    return total


def rows_kernel(y_ref, t_ref, *rest):
    out_ref = rest[-1]
    species, rows, _ = y_ref.shape
    for f in range(species + 1):
        for x in range(rows // 32):
            for at, put in ((24, 0), (0, 8)):
                here = slice(x * 32 + at, x * 32 + at + 8)
                block = y_ref[f, here, :] if f < species else t_ref[here, :]
                out_ref[f, x * 16 + put : x * 16 + put + 8, :] = block


def pack_kernel(first, y_ref, t_ref, *rest):
    out_ref = rest[-1]
    species = y_ref.shape[0]
    for f in range(species + 1):
        for h in range(2):
            rows = slice(h * 128, (h + 1) * 128)
            block = y_ref[f, rows, :] if f < species else t_ref[rows, :]
            out_ref[f, h] = block.T[first : first + EDGE]


def chemistry(shares, heat, rates):
    n = len(shares)
    speed = jnp.exp(barrier_height * (1.0 - 1.0 / heat))
    scaled = (gamma_ros * chem_step) * speed

    def production(state):
        squares = [s * s for s in state]
        return [speed * weighted(rates, i, squares) for i in range(n)]

    doubled = [2.0 * (scaled * s) for s in shares]
    factors = [
        [(1.0 if i == j else 0.0) - rates[i, j] * doubled[j] for j in range(n)] for i in range(n)
    ]
    inverse = [None] * n
    for p in range(n):
        inverse[p] = 1.0 / factors[p][p]
        for r in range(p + 1, n):
            multiplier = factors[r][p] * inverse[p]
            factors[r][p] = multiplier
            for c in range(p + 1, n):
                factors[r][c] = factors[r][c] - multiplier * factors[p][c]

    def substitute(source):
        unknown = list(source)
        for r in range(n):
            for c in range(r):
                unknown[r] = unknown[r] - factors[r][c] * unknown[c]
        for r in reversed(range(n)):
            for c in range(r + 1, n):
                unknown[r] = unknown[r] - factors[r][c] * unknown[c]
            unknown[r] = unknown[r] * inverse[r]
        return unknown

    one = substitute(production(shares))
    later = production([s + chem_step * o for s, o in zip(shares, one)])
    two = substitute([g - 2.0 * o for g, o in zip(later, one)])
    return [chem_step * (1.5 * a + 0.5 * b) for a, b in zip(one, two)]


def mixing_kernel(spread_ref, y_ref, t_ref, *rest):
    mix_ref = rest[-1]
    species = y_ref.shape[0]
    step = 32

    def body(i, carry):
        rows = pl.ds(pl.multiple_of(i * step, step), step)
        heat = t_ref[rows, :]
        heat = heat * jnp.sqrt(heat)
        shares = [y_ref[j, rows, :] for j in range(species)]
        for k in range(species):
            mix_ref[k, rows, :] = heat / (1.0 + weighted(spread_ref, k, shares))
        return carry

    lax.fori_loop(0, y_ref.shape[1] // step, body, 0)


def lane_kernel(band_ref, y_ref, mix_ref, *rest):
    acc_ref = rest[-1]

    def derivative(v):
        total = None
        for part in range(3):
            high = v.astype(jnp.bfloat16)
            term = jnp.dot(high, band_ref[...], preferred_element_type=jnp.float32)
            total = term if total is None else total + term
            v = v - high.astype(jnp.float32)
        return total

    for k in range(y_ref.shape[0]):
        flux = mix_ref[k] * (derivative(y_ref[k]) * (1.0 / 840.0))
        acc_ref[k] = (flow_step / 840.0) * derivative(flux)


def band_matrix(cells):
    band = np.zeros((cells, cells), np.float32)
    for m, weight in zip(range(1, 5), (672, -168, 32, -3)):
        for i in range(cells):
            band[(i + m) % cells, i] += weight
            band[(i - m) % cells, i] -= weight
    return jnp.asarray(band, jnp.bfloat16)


def chem_kernel(
    rate_ref, tile_ref, tally_ref, y_ref, t_ref, acc_in, acc_ref, shares_ref, heat_ref, change_ref, table_ref
):
    species = y_ref.shape[0]
    del acc_in
    member = lax.axis_index("gy") * lax.axis_size("gz") + lax.axis_index("gz")
    count = tally_ref[0, member]
    for j in range(species):
        consumed = None
        for i in range(species):
            if i != j:
                consumed = rate_ref[i, j] if consumed is None else consumed + rate_ref[i, j]
        for i in range(species):
            table_ref[i, j] = -(1.25 * consumed + rate_ref[j, j]) if i == j else rate_ref[i, j]

    def body(g, carry):
        for s in range(8):
            tile = tile_ref[0, 0, 0, g * 8 + s]
            for k in range(species):
                shares_ref[k, pl.ds(s, 1), :] = y_ref[k, pl.ds(tile, 1), :]
            heat_ref[pl.ds(s, 1), :] = t_ref[pl.ds(tile, 1), :]
        change = chemistry([shares_ref[k] for k in range(species)], heat_ref[...], table_ref)
        for k in range(species):
            change_ref[k] = change[k]
        for s in range(8):
            tile = tile_ref[0, 0, 0, g * 8 + s]

            @pl.when(g * 8 + s < count)
            def _():
                rows = [
                    acc_ref[k, pl.ds(tile, 1), :] + change_ref[k, pl.ds(s, 1), :] for k in range(species)
                ]
                for k in range(species):
                    acc_ref[k, pl.ds(tile, 1), :] = rows[k]

        return carry

    lax.fori_loop(0, (count + 7) // 8, body, 0)


def y_kernel(spread_ref, y_ref, mix_ref, other_ref, acc_in, acc_ref, pad_ref, mixpad_ref, flux_ref):
    species = y_ref.shape[0]
    del acc_in
    cells = 32

    def body(x, carry):
        base = pl.multiple_of(x * cells, cells)
        own = pl.ds(base, cells)
        for side, at in ((0, 0), (8, cells + 8)):
            rows = pl.ds(pl.multiple_of(x * 16 + side, 8), 8)
            heat = other_ref[species, rows, :]
            heat = heat * jnp.sqrt(heat)
            shares = [other_ref[j, rows, :] for j in range(species)]
            for k in range(species):
                pad_ref[k, at : at + 8, :] = shares[k]
                mixpad_ref[k, at : at + 8, :] = heat / (1.0 + weighted(spread_ref, k, shares))
        for k in range(species):
            pad_ref[k, 8 : 8 + cells, :] = y_ref[k, own, :]
            mixpad_ref[k, 8 : 8 + cells, :] = mix_ref[k, own, :]
        for k in range(species):
            slope = stencil(lambda m: pad_ref[k, 4 + m : 4 + m + cells + 8, :])
            flux_ref[k] = mixpad_ref[k, 4 : 4 + cells + 8, :] * slope
        for k in range(species):
            acc_ref[k, own, :] = acc_ref[k, own, :] + flow_step * stencil(
                lambda m: flux_ref[k, 4 + m : 4 + m + cells, :]
            )
        return carry

    lax.fori_loop(0, y_ref.shape[1] // cells, body, 0)


def z_kernel(spread_ref, low_ref, high_ref, before_ref, after_ref, acc_in, acc_ref, wide_ref, diff_ref, turn_ref):
    species = acc_ref.shape[0]
    del acc_in
    diff_ref[...] = jnp.zeros_like(diff_ref)
    turn_ref[...] = jnp.zeros_like(turn_ref)

    def fluxes(first, second, h):
        wide_ref[:, :8, :] = first[:, h]
        wide_ref[:, 8:, :] = second[:, h]
        heat = wide_ref[species, 4:12, :]
        heat = heat * jnp.sqrt(heat)
        shares = [wide_ref[j, 4:12, :] for j in range(species)]
        result = []
        for k in range(species):
            mix = heat / (1.0 + weighted(spread_ref, k, shares))
            result.append(mix * stencil(lambda m: wide_ref[k, 4 + m : 12 + m, :]))
        return result

    for h in range(2):
        wrapped = fluxes(high_ref, low_ref, h)
        for first, second, at, put in (
            (before_ref, low_ref, 12, 0),
            (high_ref, after_ref, 4, 128 - EDGE),
        ):
            true = fluxes(first, second, h)
            for k in range(species):
                diff_ref[k, 8:16, :] = true[k] - wrapped[k]
            for k in range(species):
                turn_ref[k, put : put + 8, :] = flow_step * stencil(
                    lambda m: diff_ref[k, at + m : at + m + 8, :]
                )
        for k in range(species):
            rows = slice(h * 128, (h + 1) * 128)
            acc_ref[k, rows, :] = acc_ref[k, rows, :] + turn_ref[k].T


def flux_kernel(start, y_ref, mix_ref, acc_in, before_ref, after_ref, low_ref, high_ref, acc_ref):
    del acc_in
    cells = 8

    def body(i, carry):
        k, tile = i // 4, i % 4

        def rows(x):
            return pl.ds(pl.multiple_of(x * 32 + tile * 8, 8), 8)

        line = (
            [before_ref[k, rows(x), :] for x in range(4)]
            + [y_ref[start + k, rows(x), :] for x in range(cells)]
            + [after_ref[k, rows(x), :] for x in range(4)]
        )
        flux = [
            mix_ref[start + k, rows(x), :] * stencil(lambda m: line[x + 4 + m]) for x in range(cells)
        ]
        for x in range(4):
            low_ref[k, rows(x), :] = flux[x]
            high_ref[k, rows(x), :] = flux[x + 4]
        for x in range(cells):
            total = None
            for m in range(1, 5):
                term = None
                if x + m < cells:
                    term = flux[x + m]
                if x - m >= 0:
                    term = -flux[x - m] if term is None else term - flux[x - m]
                if term is not None:
                    term = coefficients[m - 1] * term
                    total = term if total is None else total + term
            acc_ref[start + k, rows(x), :] = acc_ref[start + k, rows(x), :] + flow_step * total
        return carry

    lax.fori_loop(0, before_ref.shape[0] * 4, body, 0)


def final_kernel(start, acc_ref, before_ref, after_ref, *rest):
    out_ref, total_ref, sems = rest[-3:]
    copies = []
    for k in range(before_ref.shape[0]):
        for x in range(8):
            total = None
            for m in range(1, 5):
                if x - m < 0:
                    far = before_ref[k, (x - m + 4) * 32 : (x - m + 5) * 32, :]
                    term = -coefficients[m - 1] * far
                elif x + m >= 8:
                    far = after_ref[k, (x + m - 8) * 32 : (x + m - 7) * 32, :]
                    term = coefficients[m - 1] * far
                else:
                    continue
                total = term if total is None else total + term
            rows = slice(x * 32, (x + 1) * 32)
            total_ref[k, rows, :] = acc_ref[start + k, rows, :] + flow_step * total
        copy = pltpu.make_async_copy(total_ref.at[k], out_ref.at[start + k], sems.at[k])
        copy.start()
        copies.append(copy)
    for copy in copies:
        copy.wait()


def ring(count):
    forward = [(i, (i + 1) % count) for i in range(count)]
    return forward, [(target, source) for source, target in forward]


def shards(mass, kelvin, spreads, coupling, tiles, tally):
    species, cx, cy, cz = mass.shape
    rows = cx * cy
    whole = f32(species, rows, cz)
    y = mass.reshape(species, rows, cz)
    t = kelvin.reshape(rows, cz)
    forward_x, backward_x = ring(lax.axis_size("gx"))
    forward_y, _ = ring(lax.axis_size("gy"))
    forward_z, backward_z = ring(lax.axis_size("gz"))
    chunks = ((0, 5), (5, 4))
    half = rows // 2

    def call(kernel, name, ins, out, scratch=(), aliases=None, after=()):
        operands = [array for _, array in ins] + list(after)
        specs = [spec for spec, _ in ins] + [pl.BlockSpec(memory_space=pl.ANY)] * len(after)
        single = not isinstance(out, tuple)
        return pl.pallas_call(
            kernel,
            out_shape=out,
            in_specs=specs,
            out_specs=VMEM if single else (VMEM,) * len(out),
            scratch_shapes=list(scratch),
            input_output_aliases=aliases or {},
            compiler_params=PARAMS,
            name=name,
        )(*operands)

    halos, sent = [], []
    for start, size in chunks:
        upper, lower = y[start : start + size, half:], y[start : start + size, :half]
        sent += [upper, lower]
        halos.append(
            (lax.ppermute(upper, "gx", forward_x), lax.ppermute(lower, "gx", backward_x))
        )
    lines = f32(species + 1, cx * 16, cz)
    facing = call(rows_kernel, "facing", [(VMEM, y), (VMEM, t)], lines, after=sent)
    other = lax.ppermute(facing, "gy", forward_y)
    mix = call(
        mixing_kernel, "mixing", [(SMEM, spreads), (VMEM, y), (VMEM, t)], whole, after=[facing]
    )
    packed = f32(species + 1, 2, EDGE, 128)
    pack_high = functools.partial(pack_kernel, cz - EDGE)
    high = call(pack_high, "pack_high", [(VMEM, y), (VMEM, t)], packed, after=[other, mix])
    before_z = lax.ppermute(high, "gz", forward_z)
    acc = call(
        lane_kernel, "spanwise", [(VMEM, band_matrix(cz)), (VMEM, y), (VMEM, mix)], whole, after=[high]
    )
    low = call(
        functools.partial(pack_kernel, 0), "pack_low", [(VMEM, y), (VMEM, t)], packed, after=[before_z, acc]
    )
    after_z = lax.ppermute(low, "gz", backward_z)

    def flux(index, acc):
        start, size = chunks[index]
        before, after = halos[index]
        face = f32(size, half, cz)
        low_x, high_x, acc = call(
            functools.partial(flux_kernel, start),
            "streamwise",
            [(VMEM, y), (VMEM, mix), (VMEM, acc), (VMEM, before), (VMEM, after)],
            (face, face, whole),
            aliases={2: 2},
        )
        return acc, lax.ppermute(high_x, "gx", forward_x), lax.ppermute(low_x, "gx", backward_x)

    acc, *faces_a = flux(0, acc)
    acc = call(
        y_kernel,
        "transverse",
        [(SMEM, spreads), (VMEM, y), (VMEM, mix), (VMEM, other), (VMEM, acc)],
        whole,
        scratch=[
            pltpu.VMEM((species, cy + 16, cz), jnp.float32),
            pltpu.VMEM((species, cy + 16, cz), jnp.float32),
            pltpu.VMEM((species, cy + 8, cz), jnp.float32),
        ],
        aliases={4: 0},
    )
    acc, *faces_b = flux(1, acc)
    acc = call(
        chem_kernel,
        "chemistry",
        [(SMEM, coupling), (SMEM, tiles), (SMEM, tally), (VMEM, y), (VMEM, t), (VMEM, acc)],
        whole,
        scratch=[
            pltpu.VMEM((species, 8, cz), jnp.float32),
            pltpu.VMEM((8, cz), jnp.float32),
            pltpu.VMEM((species, 8, cz), jnp.float32),
            pltpu.SMEM((species, species), jnp.float32),
        ],
        aliases={5: 0},
    )
    acc = call(
        z_kernel,
        "faces",
        [(SMEM, spreads), (VMEM, low), (VMEM, high), (VMEM, before_z), (VMEM, after_z), (VMEM, acc)],
        whole,
        scratch=[
            pltpu.VMEM((species + 1, 16, 128), jnp.float32),
            pltpu.VMEM((species, 24, 128), jnp.float32),
            pltpu.VMEM((species, 128, 128), jnp.float32),
        ],
        aliases={5: 0},
    )
    out = None
    for (start, size), (before, after) in zip(chunks, (faces_a, faces_b)):
        operands = [acc, before, after] + ([] if out is None else [out])
        out = pl.pallas_call(
            functools.partial(final_kernel, start),
            out_shape=whole,
            in_specs=[VMEM] * 3 + [pl.BlockSpec(memory_space=pl.ANY)] * (len(operands) - 3),
            out_specs=pl.BlockSpec(memory_space=pl.ANY),
            scratch_shapes=[
                pltpu.VMEM((size, rows, cz), jnp.float32),
                pltpu.SemaphoreType.DMA((size,)),
            ],
            input_output_aliases={} if out is None else {3: 0},
            compiler_params=PARAMS,
            name="finish",
        )(*operands)
    return out.reshape(mass.shape)


def solution(mesh):
    in_specs = (
        P(None, "gx", "gy", "gz"),
        P("gx", "gy", "gz"),
        P(),
        P(),
        P("gx", "gy", "gz", None),
        P("gx", None),
    )
    out_specs = P(None, "gx", "gy", "gz")
    return jax.shard_map(shards, mesh=mesh, in_specs=in_specs, out_specs=out_specs, check_vma=False)
```

```python
import functools

import jax
import jax.numpy as jnp
import numpy as np
from jax import lax
from jax.experimental import pallas as pl
from jax.experimental.pallas import tpu as pltpu
from jax.sharding import PartitionSpec as P

SLOTS = 64
EDGE = 8
FIRST = 16
LAST = 16

coefficients = (0.8, -0.2, 4.0 / 105.0, -1.0 / 280.0)
flow_step = 0.1
chem_step = 0.1
gamma_ros = 1.0 + 0.5**0.5
barrier_height = 2.0

VMEM = pl.BlockSpec(memory_space=pltpu.VMEM)
SMEM = pl.BlockSpec(memory_space=pltpu.SMEM)
PARAMS = pltpu.CompilerParams(vmem_limit_bytes=24 * 1024 * 1024)


def f32(*shape):
    return jax.ShapeDtypeStruct(shape, jnp.float32)


def stencil(take):
    total = None
    for m in range(1, 5):
        term = coefficients[m - 1] * (take(m) - take(-m))
        total = term if total is None else total + term
    return total


def weighted(table, k, shares):
    total = table[k, 0] * shares[0]
    for j in range(1, len(shares)):
        total = total + table[k, j] * shares[j]
    return total


def facing_kernel(y_ref, t_ref, out_ref):
    species, rows, _ = y_ref.shape
    for f in range(species + 1):
        for x in range(rows // 32):
            for at, put in ((24, 0), (0, 8)):
                here = slice(x * 32 + at, x * 32 + at + 8)
                block = y_ref[f, here, :] if f < species else t_ref[here, :]
                out_ref[f, x * 16 + put : x * 16 + put + 8, :] = block


def lines_kernel(y_ref, t_ref, right_ref, left_ref):
    species = y_ref.shape[0]
    for x in range(4):
        low, high = (slice(at * 32 + FIRST, at * 32 + 32) for at in (x, x + 4))
        for k in range(species + 1):
            put = slice((k * 4 + x) * LAST, (k * 4 + x + 1) * LAST)
            if k < species:
                right_ref[put, :] = y_ref[k, low, :]
                left_ref[put, :] = y_ref[k, high, :]
            else:
                right_ref[put, :] = t_ref[high, :]
                left_ref[put, :] = t_ref[low, :]


def pack_kernel(y_ref, t_ref, low_ref, high_ref):
    species = y_ref.shape[0]
    for f in range(species + 1):
        for h in range(2):
            rows = slice(h * 128, (h + 1) * 128)
            block = y_ref[f, rows, :] if f < species else t_ref[rows, :]
            turned = block.T
            low_ref[f, h] = turned[:EDGE]
            high_ref[f, h] = turned[128 - EDGE :]


def chemistry(shares, heat, rates):
    n = len(shares)
    speed = jnp.exp(barrier_height * (1.0 - 1.0 / heat))
    scaled = (gamma_ros * chem_step) * speed

    def production(state):
        squares = [s * s for s in state]
        return [speed * weighted(rates, i, squares) for i in range(n)]

    doubled = [2.0 * (scaled * s) for s in shares]
    factors = [
        [(1.0 if i == j else 0.0) - rates[i, j] * doubled[j] for j in range(n)] for i in range(n)
    ]
    inverse = [None] * n
    for p in range(n):
        inverse[p] = 1.0 / factors[p][p]
        for r in range(p + 1, n):
            multiplier = factors[r][p] * inverse[p]
            factors[r][p] = multiplier
            for c in range(p + 1, n):
                factors[r][c] = factors[r][c] - multiplier * factors[p][c]

    def substitute(source):
        unknown = list(source)
        for r in range(n):
            for c in range(r):
                unknown[r] = unknown[r] - factors[r][c] * unknown[c]
        for r in reversed(range(n)):
            for c in range(r + 1, n):
                unknown[r] = unknown[r] - factors[r][c] * unknown[c]
            unknown[r] = unknown[r] * inverse[r]
        return unknown

    one = substitute(production(shares))
    later = production([s + chem_step * o for s, o in zip(shares, one)])
    two = substitute([g - 2.0 * o for g, o in zip(later, one)])
    return [chem_step * (1.5 * a + 0.5 * b) for a, b in zip(one, two)]


def mixing_kernel(spread_ref, y_ref, t_ref, mix_ref):
    species = y_ref.shape[0]
    step = 32

    def body(i, carry):
        rows = pl.ds(pl.multiple_of(i * step, step), step)
        heat = t_ref[rows, :]
        heat = heat * jnp.sqrt(heat)
        shares = [y_ref[j, rows, :] for j in range(species)]
        for k in range(species):
            mix_ref[k, rows, :] = heat / (1.0 + weighted(spread_ref, k, shares))
        return carry

    lax.fori_loop(0, y_ref.shape[1] // step, body, 0)


def lane_kernel(band_ref, y_ref, mix_ref, acc_ref):

    def derivative(v):
        total = None
        for part in range(3):
            high = v.astype(jnp.bfloat16)
            term = jnp.dot(high, band_ref[...], preferred_element_type=jnp.float32)
            total = term if total is None else total + term
            v = v - high.astype(jnp.float32)
        return total

    for k in range(y_ref.shape[0]):
        flux = mix_ref[k] * (derivative(y_ref[k]) * (1.0 / 840.0))
        acc_ref[k] = (flow_step / 840.0) * derivative(flux)


def band_matrix(cells):
    band = np.zeros((cells, cells), np.float32)
    for m, weight in zip(range(1, 5), (672, -168, 32, -3)):
        for i in range(cells):
            band[(i + m) % cells, i] += weight
            band[(i - m) % cells, i] -= weight
    return jnp.asarray(band, jnp.bfloat16)


def chem_kernel(
    rate_ref, tile_ref, tally_ref, y_ref, t_ref, acc_in, acc_ref, shares_ref, heat_ref, change_ref, table_ref
):
    species = y_ref.shape[0]
    del acc_in
    member = lax.axis_index("gy") * lax.axis_size("gz") + lax.axis_index("gz")
    count = tally_ref[0, member]
    for j in range(species):
        consumed = None
        for i in range(species):
            if i != j:
                consumed = rate_ref[i, j] if consumed is None else consumed + rate_ref[i, j]
        for i in range(species):
            table_ref[i, j] = -(1.25 * consumed + rate_ref[j, j]) if i == j else rate_ref[i, j]

    def body(g, carry):
        for s in range(8):
            tile = tile_ref[0, 0, 0, g * 8 + s]
            for k in range(species):
                shares_ref[k, pl.ds(s, 1), :] = y_ref[k, pl.ds(tile, 1), :]
            heat_ref[pl.ds(s, 1), :] = t_ref[pl.ds(tile, 1), :]
        change = chemistry([shares_ref[k] for k in range(species)], heat_ref[...], table_ref)
        for k in range(species):
            change_ref[k] = change[k]
        for s in range(8):
            tile = tile_ref[0, 0, 0, g * 8 + s]

            @pl.when(g * 8 + s < count)
            def _():
                rows = [
                    acc_ref[k, pl.ds(tile, 1), :] + change_ref[k, pl.ds(s, 1), :] for k in range(species)
                ]
                for k in range(species):
                    acc_ref[k, pl.ds(tile, 1), :] = rows[k]

        return carry

    lax.fori_loop(0, (count + 7) // 8, body, 0)


def y_kernel(spread_ref, y_ref, mix_ref, other_ref, acc_in, acc_ref, pad_ref, mixpad_ref, flux_ref):
    species = y_ref.shape[0]
    del acc_in
    cells = 32

    def body(x, carry):
        base = pl.multiple_of(x * cells, cells)
        own = pl.ds(base, cells)
        for side, at in ((0, 0), (8, cells + 8)):
            rows = pl.ds(pl.multiple_of(x * 16 + side, 8), 8)
            heat = other_ref[species, rows, :]
            heat = heat * jnp.sqrt(heat)
            shares = [other_ref[j, rows, :] for j in range(species)]
            for k in range(species):
                pad_ref[k, at : at + 8, :] = shares[k]
                mixpad_ref[k, at : at + 8, :] = heat / (1.0 + weighted(spread_ref, k, shares))
        for k in range(species):
            pad_ref[k, 8 : 8 + cells, :] = y_ref[k, own, :]
            mixpad_ref[k, 8 : 8 + cells, :] = mix_ref[k, own, :]
        for k in range(species):
            slope = stencil(lambda m: pad_ref[k, 4 + m : 4 + m + cells + 8, :])
            flux_ref[k] = mixpad_ref[k, 4 : 4 + cells + 8, :] * slope
        for k in range(species):
            acc_ref[k, own, :] = acc_ref[k, own, :] + flow_step * stencil(
                lambda m: flux_ref[k, 4 + m : 4 + m + cells, :]
            )
        return carry

    lax.fori_loop(0, y_ref.shape[1] // cells, body, 0)


def z_kernel(spread_ref, low_ref, high_ref, before_ref, after_ref, acc_in, acc_ref, wide_ref, diff_ref, turn_ref):
    species = acc_ref.shape[0]
    del acc_in
    diff_ref[...] = jnp.zeros_like(diff_ref)
    turn_ref[...] = jnp.zeros_like(turn_ref)

    def fluxes(first, second, h):
        wide_ref[:, :8, :] = first[:, h]
        wide_ref[:, 8:, :] = second[:, h]
        heat = wide_ref[species, 4:12, :]
        heat = heat * jnp.sqrt(heat)
        shares = [wide_ref[j, 4:12, :] for j in range(species)]
        result = []
        for k in range(species):
            mix = heat / (1.0 + weighted(spread_ref, k, shares))
            result.append(mix * stencil(lambda m: wide_ref[k, 4 + m : 12 + m, :]))
        return result

    for h in range(2):
        wrapped = fluxes(high_ref, low_ref, h)
        for first, second, at, put in (
            (before_ref, low_ref, 12, 0),
            (high_ref, after_ref, 4, 128 - EDGE),
        ):
            true = fluxes(first, second, h)
            for k in range(species):
                diff_ref[k, 8:16, :] = true[k] - wrapped[k]
            for k in range(species):
                turn_ref[k, put : put + 8, :] = flow_step * stencil(
                    lambda m: diff_ref[k, at + m : at + m + 8, :]
                )
        for k in range(species):
            rows = slice(h * 128, (h + 1) * 128)
            acc_ref[k, rows, :] = acc_ref[k, rows, :] + turn_ref[k].T


def inner(flux):
    cells = len(flux)
    result = []
    for x in range(cells):
        total = None
        for m in range(1, 5):
            term = None
            if x + m < cells:
                term = flux[x + m]
            if x - m >= 0:
                term = -flux[x - m] if term is None else term - flux[x - m]
            if term is not None:
                term = coefficients[m - 1] * term
                total = term if total is None else total + term
        result.append(total)
    return result


def first_kernel(y_ref, mix_ref, acc_in, before_ref, after_ref, low_ref, high_ref, acc_ref):
    del acc_in
    cells = 8

    def body(i, carry):
        k, tile = i // (FIRST // 8), i % (FIRST // 8)

        def rows(x, size=32):
            return pl.ds(pl.multiple_of(x * size + tile * 8, 8), 8)

        line = (
            [before_ref[k, rows(x), :] for x in range(4)]
            + [y_ref[k, rows(x), :] for x in range(cells)]
            + [after_ref[k, rows(x), :] for x in range(4)]
        )
        flux = [mix_ref[k, rows(x), :] * stencil(lambda m: line[x + 4 + m]) for x in range(cells)]
        for x in range(4):
            low_ref[k, rows(x, FIRST), :] = flux[x]
            high_ref[k, rows(x, FIRST), :] = flux[x + 4]
        for x, total in enumerate(inner(flux)):
            acc_ref[k, rows(x), :] = acc_ref[k, rows(x), :] + flow_step * total
        return carry

    lax.fori_loop(0, y_ref.shape[0] * (FIRST // 8), body, 0)


def second_kernel(
    spread_ref, y_ref, mix_ref, acc_in, before_ref, after_ref, left_ref, right_ref, acc_ref, far_ref
):
    del acc_in
    species = y_ref.shape[0]
    cells = 8

    def body(tile, carry):
        def far(ref, k, x):
            return ref[pl.ds(pl.multiple_of((k * 4 + x) * LAST + tile * 8, 8), 8), :]

        def rows(x):
            return pl.ds(pl.multiple_of(x * 32 + FIRST + tile * 8, 8), 8)

        for near_ref, ref, put in ((before_ref, left_ref, 0), (after_ref, right_ref, 4)):
            for x in range(4):
                heat = far(ref, species, x)
                heat = heat * jnp.sqrt(heat)
                shares = [near_ref[j, rows(x), :] for j in range(species)]
                for k in range(species):
                    far_ref[k, put + x] = heat / (1.0 + weighted(spread_ref, k, shares))

        def one(k, carry):
            line = (
                [far(left_ref, k, x) for x in range(4)]
                + [before_ref[k, rows(x), :] for x in range(4)]
                + [y_ref[k, rows(x), :] for x in range(cells)]
                + [after_ref[k, rows(x), :] for x in range(4)]
                + [far(right_ref, k, x) for x in range(4)]
            )
            mix = (
                [far_ref[k, x] for x in range(4)]
                + [mix_ref[k, rows(x), :] for x in range(cells)]
                + [far_ref[k, 4 + x] for x in range(4)]
            )
            flux = [mix[x] * stencil(lambda m: line[x + 4 + m]) for x in range(cells + 8)]
            for x in range(cells):
                total = stencil(lambda m: flux[x + 4 + m])
                acc_ref[k, rows(x), :] = acc_ref[k, rows(x), :] + flow_step * total
            return carry

        return lax.fori_loop(0, species, one, carry)

    lax.fori_loop(0, LAST // 8, body, 0)


def rest_kernel(acc_ref, out_ref, sems):
    copies = []
    for k in range(acc_ref.shape[0]):
        here = (k, slice(None), pl.ds(FIRST, LAST), slice(None))
        copies.append(pltpu.make_async_copy(acc_ref.at[here], out_ref.at[here], sems.at[k]))
    for copy in copies:
        copy.start()
    for copy in copies:
        copy.wait()


def final_kernel(acc_ref, before_ref, after_ref, out_in, out_ref, total_ref, sems):
    del out_in
    copies = []
    for k in range(acc_ref.shape[0]):
        for x in range(8):
            total = None
            for m in range(1, 5):
                if x - m < 0:
                    far = before_ref[k, (x - m + 4) * FIRST : (x - m + 5) * FIRST, :]
                    term = -coefficients[m - 1] * far
                elif x + m >= 8:
                    far = after_ref[k, (x + m - 8) * FIRST : (x + m - 7) * FIRST, :]
                    term = coefficients[m - 1] * far
                else:
                    continue
                total = term if total is None else total + term
            total_ref[k, x] = acc_ref[k, x, :FIRST, :] + flow_step * total
        here = (k, slice(None), pl.ds(0, FIRST), slice(None))
        copy = pltpu.make_async_copy(total_ref.at[k], out_ref.at[here], sems.at[k])
        copy.start()
        copies.append(copy)
    for copy in copies:
        copy.wait()


def ring(count):
    forward = [(i, (i + 1) % count) for i in range(count)]
    return forward, [(target, source) for source, target in forward]


def shards(mass, kelvin, spreads, coupling, tiles, tally):
    species, cx, cy, cz = mass.shape
    rows = cx * cy
    whole = f32(species, rows, cz)
    y = mass.reshape(species, rows, cz)
    t = kelvin.reshape(rows, cz)
    forward_x, backward_x = ring(lax.axis_size("gx"))
    forward_y, _ = ring(lax.axis_size("gy"))
    forward_z, backward_z = ring(lax.axis_size("gz"))
    def call(kernel, name, ins, out, scratch=(), aliases=None, after=(), params=PARAMS):
        operands = [array for _, array in ins] + list(after)
        specs = [spec for spec, _ in ins] + [pl.BlockSpec(memory_space=pl.ANY)] * len(after)
        single = not isinstance(out, tuple)

        def body(*refs):
            kernel(*refs[: len(ins)], *refs[len(operands) :])

        return pl.pallas_call(
            body,
            out_shape=out,
            in_specs=specs,
            out_specs=VMEM if single else (VMEM,) * len(out),
            scratch_shapes=list(scratch),
            input_output_aliases=aliases or {},
            compiler_params=params,
            name=name,
        )(*operands)

    far = f32((species + 1) * 4 * LAST, cz)
    in_hbm = pl.BlockSpec(memory_space=pl.ANY)
    upper, lower = y[:, 4 * cy :], y[:, : 4 * cy]
    before = lax.ppermute(upper, "gx", forward_x)
    after = lax.ppermute(lower, "gx", backward_x)
    facing = call(
        facing_kernel, "facing", [(VMEM, y), (VMEM, t)], f32(species + 1, cx * 16, cz), after=[upper, lower]
    )
    other = lax.ppermute(facing, "gy", forward_y)
    packed = f32(species + 1, 2, EDGE, 128)
    low, high = call(pack_kernel, "pack", [(VMEM, y), (VMEM, t)], (packed, packed), after=[facing])
    before_z = lax.ppermute(high, "gz", forward_z)
    after_z = lax.ppermute(low, "gz", backward_z)
    mix = call(mixing_kernel, "mixing", [(SMEM, spreads), (VMEM, y), (VMEM, t)], whole, after=[high])
    acc = call(lane_kernel, "spanwise", [(VMEM, band_matrix(cz)), (VMEM, y), (VMEM, mix)], whole)
    far = f32((species + 1) * 4 * LAST, cz)
    right, left = call(lines_kernel, "lines", [(VMEM, y), (VMEM, t)], (far, far), after=[acc])
    before_b = lax.ppermute(right, "gx", forward_x)
    after_b = lax.ppermute(left, "gx", backward_x)
    acc = call(
        y_kernel,
        "transverse",
        [(SMEM, spreads), (VMEM, y), (VMEM, mix), (VMEM, other), (VMEM, acc)],
        whole,
        scratch=[
            pltpu.VMEM((species, cy + 16, cz), jnp.float32),
            pltpu.VMEM((species, cy + 16, cz), jnp.float32),
            pltpu.VMEM((species, cy + 8, cz), jnp.float32),
        ],
        aliases={4: 0},
        after=[right],
    )
    acc = call(
        z_kernel,
        "faces",
        [(SMEM, spreads), (VMEM, low), (VMEM, high), (VMEM, before_z), (VMEM, after_z), (VMEM, acc)],
        whole,
        scratch=[
            pltpu.VMEM((species + 1, 16, 128), jnp.float32),
            pltpu.VMEM((species, 24, 128), jnp.float32),
            pltpu.VMEM((species, 128, 128), jnp.float32),
        ],
        aliases={5: 0},
    )
    edge = f32(species, 4 * FIRST, cz)
    low_x, high_x, acc = call(
        first_kernel,
        "streamwise",
        [(VMEM, y), (VMEM, mix), (VMEM, acc), (VMEM, before), (VMEM, after)],
        (edge, edge, whole),
        after=[high],
        aliases={2: 2},
    )
    before_a = lax.ppermute(high_x, "gx", forward_x)
    after_a = lax.ppermute(low_x, "gx", backward_x)
    acc = call(
        chem_kernel,
        "chemistry",
        [(SMEM, coupling), (SMEM, tiles), (SMEM, tally), (VMEM, y), (VMEM, t), (VMEM, acc)],
        whole,
        scratch=[
            pltpu.VMEM((species, 8, cz), jnp.float32),
            pltpu.VMEM((8, cz), jnp.float32),
            pltpu.VMEM((species, 8, cz), jnp.float32),
            pltpu.SMEM((species, species), jnp.float32),
        ],
        aliases={5: 0},
    )
    acc = call(
        second_kernel,
        "neighbours",
        [(SMEM, spreads)] + [(VMEM, v) for v in (y, mix, acc, before, after, before_b, after_b)],
        whole,
        scratch=[pltpu.VMEM((species, 8, 8, cz), jnp.float32)],
        aliases={3: 0},
    )
    acc = acc.reshape(mass.shape)
    result = f32(*mass.shape)
    out = pl.pallas_call(
        rest_kernel,
        out_shape=result,
        in_specs=[VMEM],
        out_specs=in_hbm,
        scratch_shapes=[pltpu.SemaphoreType.DMA((species,))],
        compiler_params=PARAMS,
        name="rest",
    )(acc)
    return pl.pallas_call(
        final_kernel,
        out_shape=result,
        in_specs=[VMEM] * 3 + [in_hbm],
        out_specs=in_hbm,
        scratch_shapes=[
            pltpu.VMEM((species, cx, FIRST, cz), jnp.float32),
            pltpu.SemaphoreType.DMA((species,)),
        ],
        input_output_aliases={3: 0},
        compiler_params=PARAMS,
        name="finish",
    )(acc, before_a, after_a, out)


def solution(mesh):
    in_specs = (
        P(None, "gx", "gy", "gz"),
        P("gx", "gy", "gz"),
        P(),
        P(),
        P("gx", "gy", "gz", None),
        P("gx", None),
    )
    out_specs = P(None, "gx", "gy", "gz")
    return jax.shard_map(shards, mesh=mesh, in_specs=in_specs, out_specs=out_specs, check_vma=False)
```

```python
import functools

import jax
import jax.numpy as jnp
import numpy as np
from jax import lax
from jax.experimental import pallas as pl
from jax.experimental.pallas import tpu as pltpu
from jax.sharding import PartitionSpec as P

SLOTS = 64
EDGE = 8
WIDE = 75
FIRST = 16
LAST = 16

coefficients = (0.8, -0.2, 4.0 / 105.0, -1.0 / 280.0)
flow_step = 0.1
chem_step = 0.1
gamma_ros = 1.0 + 0.5**0.5
barrier_height = 2.0

VMEM = pl.BlockSpec(memory_space=pltpu.VMEM)
SMEM = pl.BlockSpec(memory_space=pltpu.SMEM)
PARAMS = pltpu.CompilerParams(vmem_limit_bytes=24 * 1024 * 1024)


def f32(*shape):
    return jax.ShapeDtypeStruct(shape, jnp.float32)


def stencil(take):
    total = None
    for m in range(1, 5):
        term = coefficients[m - 1] * (take(m) - take(-m))
        total = term if total is None else total + term
    return total


def weighted(table, k, shares):
    total = table[k, 0] * shares[0]
    for j in range(1, len(shares)):
        total = total + table[k, j] * shares[j]
    return total


def facing_rows(put_ref, f, source):
    for x in range(8):
        for at, put in ((24, 0), (0, 8)):
            put_ref[f, x * 16 + put : x * 16 + put + 8, :] = source[x * 32 + at : x * 32 + at + 8, :]


def facing_kernel(y_ref, out_ref):
    for f in range(out_ref.shape[0]):
        facing_rows(out_ref, f, y_ref.at[f])


def warm_kernel(y_ref, t_ref, out_ref):
    facing_rows(out_ref, 0, y_ref.at[y_ref.shape[0] - 1])
    facing_rows(out_ref, 1, t_ref)


def lines_kernel(y_ref, t_ref, right_ref, left_ref):
    species = y_ref.shape[0]
    for x in range(4):
        low, high = (slice(at * 32 + FIRST, at * 32 + 32) for at in (x, x + 4))
        for k in range(species + 1):
            put = slice((k * 4 + x) * LAST, (k * 4 + x + 1) * LAST)
            if k < species:
                right_ref[put, :] = y_ref[k, low, :]
                left_ref[put, :] = y_ref[k, high, :]
            else:
                right_ref[put, :] = t_ref[high, :]
                left_ref[put, :] = t_ref[low, :]


def pack_kernel(y_ref, t_ref, low_ref, high_ref):
    species = y_ref.shape[0]
    for f in range(species + 1):
        for h in range(2):
            rows = slice(h * 128, (h + 1) * 128)
            block = y_ref[f, rows, :] if f < species else t_ref[rows, :]
            turned = block.T
            low_ref[2 * f + h] = turned[:EDGE]
            high_ref[2 * f + h] = turned[128 - EDGE :]


def extend_kernel(low_ref, wide_ref):
    used = low_ref.shape[0]
    wide_ref[:used] = low_ref[...]
    wide_ref[used:] = jnp.zeros((WIDE - used, EDGE, 128), jnp.float32)


def chemistry(shares, heat, rates):
    n = len(shares)
    speed = jnp.exp(barrier_height * (1.0 - 1.0 / heat))
    scaled = (gamma_ros * chem_step) * speed

    def production(state):
        squares = [s * s for s in state]
        return [speed * weighted(rates, i, squares) for i in range(n)]

    doubled = [2.0 * (scaled * s) for s in shares]
    factors = [
        [(1.0 if i == j else 0.0) - rates[i, j] * doubled[j] for j in range(n)] for i in range(n)
    ]
    inverse = [None] * n
    for p in range(n):
        inverse[p] = 1.0 / factors[p][p]
        for r in range(p + 1, n):
            multiplier = factors[r][p] * inverse[p]
            factors[r][p] = multiplier
            for c in range(p + 1, n):
                factors[r][c] = factors[r][c] - multiplier * factors[p][c]

    def substitute(source):
        unknown = list(source)
        for r in range(n):
            for c in range(r):
                unknown[r] = unknown[r] - factors[r][c] * unknown[c]
        for r in reversed(range(n)):
            for c in range(r + 1, n):
                unknown[r] = unknown[r] - factors[r][c] * unknown[c]
            unknown[r] = unknown[r] * inverse[r]
        return unknown

    one = substitute(production(shares))
    later = production([s + chem_step * o for s, o in zip(shares, one)])
    two = substitute([g - 2.0 * o for g, o in zip(later, one)])
    return [chem_step * (1.5 * a + 0.5 * b) for a, b in zip(one, two)]


def mixing_kernel(spread_ref, y_ref, t_ref, mix_ref):
    species = y_ref.shape[0]
    step = 32

    def body(i, carry):
        rows = pl.ds(pl.multiple_of(i * step, step), step)
        heat = t_ref[rows, :]
        heat = heat * jnp.sqrt(heat)
        shares = [y_ref[j, rows, :] for j in range(species)]
        for k in range(species):
            mix_ref[k, rows, :] = heat / (1.0 + weighted(spread_ref, k, shares))
        return carry

    lax.fori_loop(0, y_ref.shape[1] // step, body, 0)


def split(v):
    parts = []
    for _ in range(3):
        part = v.astype(jnp.bfloat16)
        v = v - part.astype(jnp.float32)
        parts.append(part)
    return parts


def lane_kernel(band_ref, y_ref, mix_ref, acc_ref):

    def derivative(v):
        total = None
        for part in split(v):
            term = jnp.dot(part, band_ref[...], preferred_element_type=jnp.float32)
            total = term if total is None else total + term
        return total

    for k in range(y_ref.shape[0]):
        flux = mix_ref[k] * (derivative(y_ref[k]) * (1.0 / 840.0))
        acc_ref[k] = (flow_step / 840.0) * derivative(flux)


def band_matrix(cells):
    band = np.zeros((cells, cells), np.float32)
    for m, weight in zip(range(1, 5), (672, -168, 32, -3)):
        for i in range(cells):
            band[(i + m) % cells, i] += weight
            band[(i - m) % cells, i] -= weight
    return jnp.asarray(band, jnp.bfloat16)


def chem_kernel(
    rate_ref, tile_ref, tally_ref, y_ref, t_ref, acc_in, acc_ref, shares_ref, heat_ref, change_ref, table_ref
):
    species = y_ref.shape[0]
    del acc_in
    member = lax.axis_index("gy") * lax.axis_size("gz") + lax.axis_index("gz")
    count = tally_ref[0, member]
    for j in range(species):
        consumed = None
        for i in range(species):
            if i != j:
                consumed = rate_ref[i, j] if consumed is None else consumed + rate_ref[i, j]
        for i in range(species):
            table_ref[i, j] = -(1.25 * consumed + rate_ref[j, j]) if i == j else rate_ref[i, j]

    def body(g, carry):
        for s in range(8):
            tile = tile_ref[0, 0, 0, g * 8 + s]
            for k in range(species):
                shares_ref[k, pl.ds(s, 1), :] = y_ref[k, pl.ds(tile, 1), :]
            heat_ref[pl.ds(s, 1), :] = t_ref[pl.ds(tile, 1), :]
        change = chemistry([shares_ref[k] for k in range(species)], heat_ref[...], table_ref)
        live = g * 8 + lax.broadcasted_iota(jnp.int32, heat_ref.shape, 0) < count
        for k in range(species):
            change_ref[k] = jnp.where(live, change[k], 0.0)
        for s in range(8):
            row = pl.ds(tile_ref[0, 0, 0, g * 8 + s], 1)
            rows = [acc_ref[k, row, :] + change_ref[k, pl.ds(s, 1), :] for k in range(species)]
            for k in range(species):
                acc_ref[k, row, :] = rows[k]
        return carry

    lax.fori_loop(0, (count + 7) // 8, body, 0)


def split(v):
    parts = []
    for _ in range(3):
        part = v.astype(jnp.bfloat16)
        v = v - part.astype(jnp.float32)
        parts.append(part)
    return parts


def y_kernel(
    spread_ref, y_ref, mix_ref, other_ref, warm_ref, acc_in, acc_ref, pad_ref, mixpad_ref, flux_ref
):
    species = y_ref.shape[0]
    del acc_in
    cells = 32

    def body(x, carry):
        base = pl.multiple_of(x * cells, cells)
        own = pl.ds(base, cells)
        for side, at in ((0, 0), (8, cells + 8)):
            rows = pl.ds(pl.multiple_of(x * 16 + side, 8), 8)
            heat = warm_ref[1, rows, :]
            heat = heat * jnp.sqrt(heat)
            shares = [other_ref[j, rows, :] for j in range(species - 1)] + [warm_ref[0, rows, :]]
            for k in range(species):
                pad_ref[k, at : at + 8, :] = shares[k]
                mixpad_ref[k, at : at + 8, :] = heat / (1.0 + weighted(spread_ref, k, shares))
        for k in range(species):
            pad_ref[k, 8 : 8 + cells, :] = y_ref[k, own, :]
            mixpad_ref[k, 8 : 8 + cells, :] = mix_ref[k, own, :]
        for k in range(species):
            slope = stencil(lambda m: pad_ref[k, 4 + m : 4 + m + cells + 8, :])
            flux_ref[k] = mixpad_ref[k, 4 : 4 + cells + 8, :] * slope
        for k in range(species):
            acc_ref[k, own, :] = acc_ref[k, own, :] + flow_step * stencil(
                lambda m: flux_ref[k, 4 + m : 4 + m + cells, :]
            )
        return carry

    lax.fori_loop(0, y_ref.shape[1] // cells, body, 0)


def z_kernel(spread_ref, low_ref, high_ref, before_ref, after_ref, acc_in, acc_ref, wide_ref, diff_ref, turn_ref):
    species = acc_ref.shape[0]
    del acc_in
    diff_ref[...] = jnp.zeros_like(diff_ref)
    turn_ref[...] = jnp.zeros_like(turn_ref)

    def fluxes(first, second, h):
        for f in range(species + 1):
            wide_ref[f, :8, :] = first[2 * f + h]
            wide_ref[f, 8:, :] = second[2 * f + h]
        heat = wide_ref[species, 4:12, :]
        heat = heat * jnp.sqrt(heat)
        shares = [wide_ref[j, 4:12, :] for j in range(species)]
        result = []
        for k in range(species):
            mix = heat / (1.0 + weighted(spread_ref, k, shares))
            result.append(mix * stencil(lambda m: wide_ref[k, 4 + m : 12 + m, :]))
        return result

    for h in range(2):
        wrapped = fluxes(high_ref, low_ref, h)
        for first, second, at, put in (
            (before_ref, low_ref, 12, 0),
            (high_ref, after_ref, 4, 128 - EDGE),
        ):
            true = fluxes(first, second, h)
            for k in range(species):
                diff_ref[k, 8:16, :] = true[k] - wrapped[k]
            for k in range(species):
                turn_ref[k, put : put + 8, :] = flow_step * stencil(
                    lambda m: diff_ref[k, at + m : at + m + 8, :]
                )
        for k in range(species):
            rows = slice(h * 128, (h + 1) * 128)
            acc_ref[k, rows, :] = acc_ref[k, rows, :] + turn_ref[k].T


def inner(flux):
    cells = len(flux)
    result = []
    for x in range(cells):
        total = None
        for m in range(1, 5):
            term = None
            if x + m < cells:
                term = flux[x + m]
            if x - m >= 0:
                term = -flux[x - m] if term is None else term - flux[x - m]
            if term is not None:
                term = coefficients[m - 1] * term
                total = term if total is None else total + term
        result.append(total)
    return result


def first_kernel(y_ref, mix_ref, acc_in, before_ref, after_ref, low_ref, high_ref, acc_ref):
    del acc_in
    cells = 8

    def body(i, carry):
        k, tile = i // (FIRST // 8), i % (FIRST // 8)

        def rows(x, size=32):
            return pl.ds(pl.multiple_of(x * size + tile * 8, 8), 8)

        line = (
            [before_ref[k, rows(x), :] for x in range(4)]
            + [y_ref[k, rows(x), :] for x in range(cells)]
            + [after_ref[k, rows(x), :] for x in range(4)]
        )
        flux = [mix_ref[k, rows(x), :] * stencil(lambda m: line[x + 4 + m]) for x in range(cells)]
        for x in range(4):
            low_ref[k, rows(x, FIRST), :] = flux[x]
            high_ref[k, rows(x, FIRST), :] = flux[x + 4]
        for x, total in enumerate(inner(flux)):
            acc_ref[k, rows(x), :] = acc_ref[k, rows(x), :] + flow_step * total
        return carry

    lax.fori_loop(0, y_ref.shape[0] * (FIRST // 8), body, 0)


def second_kernel(
    spread_ref, y_ref, mix_ref, acc_in, before_ref, after_ref, left_ref, right_ref,
    acc_ref, out_ref, far_ref, sems,
):
    del acc_in
    species = y_ref.shape[0]
    cells, tiles = 8, LAST // 8

    def far(ref, k, x, tile):
        return ref[pl.ds(pl.multiple_of((k * 4 + x) * LAST + tile * 8, 8), 8), :]

    def rows(x, tile):
        return pl.ds(pl.multiple_of(x * 32 + FIRST + tile * 8, 8), 8)

    def mixing(tile, carry):
        for near_ref, ref, put in ((before_ref, left_ref, 0), (after_ref, right_ref, 4)):
            heats = [far(ref, species, x, tile) for x in range(4)]
            heats = [heat * jnp.sqrt(heat) for heat in heats]
            shares = [[near_ref[j, rows(x, tile), :] for j in range(species)] for x in range(4)]
            for k in range(species):
                weights = [spread_ref[k, j] for j in range(species)]
                for x in range(4):
                    total = 1.0
                    for weight, share in zip(weights, shares[x]):
                        total = total + weight * share
                    far_ref[tile, k, put + x] = heats[x] / total
        return carry

    lax.fori_loop(0, tiles, mixing, 0)

    def copy(k):
        here = (k, slice(None), pl.ds(FIRST, LAST), slice(None))
        return pltpu.make_async_copy(acc_ref.at[here], out_ref.at[here], sems.at[k])

    def one(k, carry):
        for tile in range(tiles):
            line = (
                [far(left_ref, k, x, tile) for x in range(4)]
                + [before_ref[k, rows(x, tile), :] for x in range(4)]
                + [y_ref[k, rows(x, tile), :] for x in range(cells)]
                + [after_ref[k, rows(x, tile), :] for x in range(4)]
                + [far(right_ref, k, x, tile) for x in range(4)]
            )
            mix = (
                [far_ref[tile, k, x] for x in range(4)]
                + [mix_ref[k, rows(x, tile), :] for x in range(cells)]
                + [far_ref[tile, k, 4 + x] for x in range(4)]
            )
            flux = [mix[x] * stencil(lambda m: line[x + 4 + m]) for x in range(cells + 8)]
            here = slice(FIRST + tile * 8, FIRST + tile * 8 + 8)
            for x in range(cells):
                total = stencil(lambda m: flux[x + 4 + m])
                acc_ref[k, x, here, :] = acc_ref[k, x, here, :] + flow_step * total
        copy(k).start()
        return carry

    lax.fori_loop(0, species, one, 0)
    lax.fori_loop(0, species, lambda k, carry: (copy(k).wait(), carry)[1], 0)


def final_kernel(acc_ref, before_ref, after_ref, out_in, out_ref, total_ref, sems):
    del out_in
    copies = []
    for k in range(acc_ref.shape[0]):
        for x in range(8):
            total = None
            for m in range(1, 5):
                if x - m < 0:
                    far = before_ref[k, (x - m + 4) * FIRST : (x - m + 5) * FIRST, :]
                    term = -coefficients[m - 1] * far
                elif x + m >= 8:
                    far = after_ref[k, (x + m - 8) * FIRST : (x + m - 7) * FIRST, :]
                    term = coefficients[m - 1] * far
                else:
                    continue
                total = term if total is None else total + term
            total_ref[k, x] = acc_ref[k, x, :FIRST, :] + flow_step * total
        here = (k, slice(None), pl.ds(0, FIRST), slice(None))
        copy = pltpu.make_async_copy(total_ref.at[k], out_ref.at[here], sems.at[k])
        copy.start()
        copies.append(copy)
    for copy in copies:
        copy.wait()


def ring(count):
    forward = [(i, (i + 1) % count) for i in range(count)]
    return forward, [(target, source) for source, target in forward]


def shards(mass, kelvin, spreads, coupling, tiles, tally):
    species, cx, cy, cz = mass.shape
    rows = cx * cy
    whole = f32(species, rows, cz)
    y = mass.reshape(species, rows, cz)
    t = kelvin.reshape(rows, cz)
    forward_x, backward_x = ring(lax.axis_size("gx"))
    forward_y, _ = ring(lax.axis_size("gy"))
    forward_z, backward_z = ring(lax.axis_size("gz"))

    def call(kernel, name, ins, out, scratch=(), aliases=None, after=(), params=PARAMS):
        operands = [array for _, array in ins] + list(after)
        specs = [spec for spec, _ in ins] + [pl.BlockSpec(memory_space=pl.ANY)] * len(after)
        single = not isinstance(out, tuple)

        def body(*refs):
            kernel(*refs[: len(ins)], *refs[len(operands) :])

        return pl.pallas_call(
            body,
            out_shape=out,
            in_specs=specs,
            out_specs=VMEM if single else (VMEM,) * len(out),
            scratch_shapes=list(scratch),
            input_output_aliases=aliases or {},
            compiler_params=params,
            name=name,
        )(*operands)

    in_hbm = pl.BlockSpec(memory_space=pl.ANY)
    upper, lower = y[:, 4 * cy :], y[:, : 4 * cy]
    before = lax.ppermute(upper, "gx", forward_x)
    after = lax.ppermute(lower, "gx", backward_x)
    facing = call(facing_kernel, "facing", [(VMEM, y)], f32(species - 1, cx * 16, cz), after=[lower, upper])
    other = lax.ppermute(facing, "gy", forward_y)
    warm = call(warm_kernel, "warm", [(VMEM, y), (VMEM, t)], f32(2, cx * 16, cz), after=[facing])
    other_t = lax.ppermute(warm, "gy", forward_y)
    packed = f32(2 * species + 2, EDGE, 128)
    low, high = call(pack_kernel, "pack", [(VMEM, y), (VMEM, t)], (packed, packed), after=[facing])
    before_z = lax.ppermute(high, "gz", forward_z)
    mix = call(mixing_kernel, "mixing", [(SMEM, spreads), (VMEM, y), (VMEM, t)], whole, after=[low, high])
    acc = call(lane_kernel, "spanwise", [(VMEM, band_matrix(cz)), (VMEM, y), (VMEM, mix)], whole)
    far = f32((species + 1) * 4 * LAST, cz)
    right, left = call(lines_kernel, "lines", [(VMEM, y), (VMEM, t)], (far, far), after=[acc])
    before_b = lax.ppermute(right, "gx", forward_x)
    after_b = lax.ppermute(left, "gx", backward_x)
    wide = call(extend_kernel, "extend", [(VMEM, low)], f32(WIDE, EDGE, 128), after=[left, right, before_z])
    after_z = lax.ppermute(wide, "gz", backward_z)
    acc = call(
        y_kernel,
        "transverse",
        [(SMEM, spreads)] + [(VMEM, v) for v in (y, mix, other, other_t, acc)],
        whole,
        scratch=[
            pltpu.VMEM((species, cy + 16, cz), jnp.float32),
            pltpu.VMEM((species, cy + 16, cz), jnp.float32),
            pltpu.VMEM((species, cy + 8, cz), jnp.float32),
        ],
        aliases={5: 0},
        after=[wide],
    )
    edge = f32(species, 4 * FIRST, cz)
    low_x, high_x, acc = call(
        first_kernel,
        "streamwise",
        [(VMEM, v) for v in (y, mix, acc, before, after)],
        (edge, edge, whole),
        aliases={2: 2},
        after=[],
    )
    before_a = lax.ppermute(high_x, "gx", forward_x)
    after_a = lax.ppermute(low_x, "gx", backward_x)
    acc = call(
        chem_kernel,
        "chemistry",
        [(SMEM, coupling), (SMEM, tiles), (SMEM, tally), (VMEM, y), (VMEM, t), (VMEM, acc)],
        whole,
        scratch=[
            pltpu.VMEM((species, 8, cz), jnp.float32),
            pltpu.VMEM((8, cz), jnp.float32),
            pltpu.VMEM((species, 8, cz), jnp.float32),
            pltpu.SMEM((species, species), jnp.float32),
        ],
        aliases={5: 0},
    )
    acc = call(
        z_kernel,
        "faces",
        [(SMEM, spreads)] + [(VMEM, v) for v in (low, high, before_z, after_z, acc)],
        whole,
        scratch=[
            pltpu.VMEM((species + 1, 16, 128), jnp.float32),
            pltpu.VMEM((species, 24, 128), jnp.float32),
            pltpu.VMEM((species, 128, 128), jnp.float32),
        ],
        aliases={5: 0},
    )
    result = f32(*mass.shape)
    acc, out = pl.pallas_call(
        second_kernel,
        out_shape=(result, result),
        in_specs=[SMEM] + [VMEM] * 7,
        out_specs=(VMEM, in_hbm),
        scratch_shapes=[
            pltpu.VMEM((LAST // 8, species, 8, 8, cz), jnp.float32),
            pltpu.SemaphoreType.DMA((species,)),
        ],
        input_output_aliases={3: 0},
        compiler_params=PARAMS,
        name="neighbours",
    )(spreads, y, mix, acc.reshape(mass.shape), before, after, before_b, after_b)
    return pl.pallas_call(
        final_kernel,
        out_shape=result,
        in_specs=[VMEM] * 3 + [in_hbm],
        out_specs=in_hbm,
        scratch_shapes=[
            pltpu.VMEM((species, cx, FIRST, cz), jnp.float32),
            pltpu.SemaphoreType.DMA((species,)),
        ],
        input_output_aliases={3: 0},
        compiler_params=PARAMS,
        name="finish",
    )(acc, before_a, after_a, out)


def solution(mesh):
    in_specs = (
        P(None, "gx", "gy", "gz"),
        P("gx", "gy", "gz"),
        P(),
        P(),
        P("gx", "gy", "gz", None),
        P("gx", None),
    )
    out_specs = P(None, "gx", "gy", "gz")
    return jax.shard_map(shards, mesh=mesh, in_specs=in_specs, out_specs=out_specs, check_vma=False)
```

```python
import functools

import jax
import jax.numpy as jnp
import numpy as np
from jax import lax
from jax.experimental import pallas as pl
from jax.experimental.pallas import tpu as pltpu
from jax.sharding import PartitionSpec as P

SLOTS = 64
EDGE = 8
WIDE = 75
FIRST = 16
LAST = 16

coefficients = (0.8, -0.2, 4.0 / 105.0, -1.0 / 280.0)
flow_step = 0.1
chem_step = 0.1
gamma_ros = 1.0 + 0.5**0.5
barrier_height = 2.0

VMEM = pl.BlockSpec(memory_space=pltpu.VMEM)
SMEM = pl.BlockSpec(memory_space=pltpu.SMEM)
PARAMS = pltpu.CompilerParams(vmem_limit_bytes=24 * 1024 * 1024)


def f32(*shape):
    return jax.ShapeDtypeStruct(shape, jnp.float32)


def stencil(take):
    total = None
    for m in range(1, 5):
        term = coefficients[m - 1] * (take(m) - take(-m))
        total = term if total is None else total + term
    return total


def weighted(table, k, shares):
    total = table[k, 0] * shares[0]
    for j in range(1, len(shares)):
        total = total + table[k, j] * shares[j]
    return total


def facing_rows(put_ref, f, source):
    for x in range(8):
        for at, put in ((24, 0), (0, 8)):
            put_ref[f, x * 16 + put : x * 16 + put + 8, :] = source[x * 32 + at : x * 32 + at + 8, :]


def facing_kernel(y_ref, out_ref):
    for f in range(out_ref.shape[0]):
        facing_rows(out_ref, f, y_ref.at[f])


def warm_kernel(y_ref, t_ref, out_ref):
    facing_rows(out_ref, 0, y_ref.at[y_ref.shape[0] - 1])
    facing_rows(out_ref, 1, t_ref)


def lines_kernel(y_ref, t_ref, right_ref, left_ref):
    species = y_ref.shape[0]
    for x in range(4):
        low, high = (slice(at * 32 + FIRST, at * 32 + 32) for at in (x, x + 4))
        for k in range(species + 1):
            put = slice((k * 4 + x) * LAST, (k * 4 + x + 1) * LAST)
            if k < species:
                right_ref[put, :] = y_ref[k, low, :]
                left_ref[put, :] = y_ref[k, high, :]
            else:
                right_ref[put, :] = t_ref[high, :]
                left_ref[put, :] = t_ref[low, :]


def pack_kernel(y_ref, t_ref, low_ref, high_ref):
    species = y_ref.shape[0]
    for f in range(species + 1):
        for h in range(2):
            rows = slice(h * 128, (h + 1) * 128)
            block = y_ref[f, rows, :] if f < species else t_ref[rows, :]
            turned = block.T
            low_ref[2 * f + h] = turned[:EDGE]
            high_ref[2 * f + h] = turned[128 - EDGE :]


def extend_kernel(low_ref, wide_ref):
    used = low_ref.shape[0]
    wide_ref[:used] = low_ref[...]
    wide_ref[used:] = jnp.zeros((WIDE - used, EDGE, 128), jnp.float32)


def chemistry(shares, heat, rates):
    n = len(shares)
    speed = jnp.exp(barrier_height * (1.0 - 1.0 / heat))
    scaled = (gamma_ros * chem_step) * speed

    def production(state):
        squares = [s * s for s in state]
        return [speed * weighted(rates, i, squares) for i in range(n)]

    doubled = [2.0 * (scaled * s) for s in shares]
    factors = [
        [(1.0 if i == j else 0.0) - rates[i, j] * doubled[j] for j in range(n)] for i in range(n)
    ]
    inverse = [None] * n
    for p in range(n):
        inverse[p] = 1.0 / factors[p][p]
        for r in range(p + 1, n):
            multiplier = factors[r][p] * inverse[p]
            factors[r][p] = multiplier
            for c in range(p + 1, n):
                factors[r][c] = factors[r][c] - multiplier * factors[p][c]

    def substitute(source):
        unknown = list(source)
        for r in range(n):
            for c in range(r):
                unknown[r] = unknown[r] - factors[r][c] * unknown[c]
        for r in reversed(range(n)):
            for c in range(r + 1, n):
                unknown[r] = unknown[r] - factors[r][c] * unknown[c]
            unknown[r] = unknown[r] * inverse[r]
        return unknown

    one = substitute(production(shares))
    later = production([s + chem_step * o for s, o in zip(shares, one)])
    two = substitute([g - 2.0 * o for g, o in zip(later, one)])
    return [chem_step * (1.5 * a + 0.5 * b) for a, b in zip(one, two)]


def mixing_kernel(spread_ref, y_ref, t_ref, mix_ref):
    species = y_ref.shape[0]
    step = 32

    def body(i, carry):
        rows = pl.ds(pl.multiple_of(i * step, step), step)
        heat = t_ref[rows, :]
        heat = heat * jnp.sqrt(heat)
        shares = [y_ref[j, rows, :] for j in range(species)]
        for k in range(species):
            mix_ref[k, rows, :] = heat / (1.0 + weighted(spread_ref, k, shares))
        return carry

    lax.fori_loop(0, y_ref.shape[1] // step, body, 0)


def split(v):
    parts = []
    for _ in range(3):
        part = v.astype(jnp.bfloat16)
        v = v - part.astype(jnp.float32)
        parts.append(part)
    return parts


def lane_kernel(band_ref, y_ref, mix_ref, acc_ref):

    def derivative(v):
        total = None
        for part in split(v):
            term = jnp.dot(part, band_ref[...], preferred_element_type=jnp.float32)
            total = term if total is None else total + term
        return total

    for k in range(y_ref.shape[0]):
        flux = mix_ref[k] * (derivative(y_ref[k]) * (1.0 / 840.0))
        acc_ref[k] = (flow_step / 840.0) * derivative(flux)


def band_matrix(cells):
    band = np.zeros((cells, cells), np.float32)
    for m, weight in zip(range(1, 5), (672, -168, 32, -3)):
        for i in range(cells):
            band[(i + m) % cells, i] += weight
            band[(i - m) % cells, i] -= weight
    return jnp.asarray(band, jnp.bfloat16)


def chem_kernel(
    rate_ref, tile_ref, tally_ref, y_ref, t_ref, acc_in, acc_ref, shares_ref, heat_ref, change_ref, table_ref
):
    species = y_ref.shape[0]
    del acc_in
    member = lax.axis_index("gy") * lax.axis_size("gz") + lax.axis_index("gz")
    count = tally_ref[0, member]
    for j in range(species):
        consumed = None
        for i in range(species):
            if i != j:
                consumed = rate_ref[i, j] if consumed is None else consumed + rate_ref[i, j]
        for i in range(species):
            table_ref[i, j] = -(1.25 * consumed + rate_ref[j, j]) if i == j else rate_ref[i, j]

    def body(g, carry):
        for s in range(8):
            tile = tile_ref[0, 0, 0, g * 8 + s]
            for k in range(species):
                shares_ref[k, pl.ds(s, 1), :] = y_ref[k, pl.ds(tile, 1), :]
            heat_ref[pl.ds(s, 1), :] = t_ref[pl.ds(tile, 1), :]
        change = chemistry([shares_ref[k] for k in range(species)], heat_ref[...], table_ref)
        live = g * 8 + lax.broadcasted_iota(jnp.int32, heat_ref.shape, 0) < count
        for k in range(species):
            change_ref[k] = jnp.where(live, change[k], 0.0)
        for s in range(8):
            row = pl.ds(tile_ref[0, 0, 0, g * 8 + s], 1)
            rows = [acc_ref[k, row, :] + change_ref[k, pl.ds(s, 1), :] for k in range(species)]
            for k in range(species):
                acc_ref[k, row, :] = rows[k]
        return carry

    lax.fori_loop(0, (count + 7) // 8, body, 0)


def split(v):
    parts = []
    for _ in range(3):
        part = v.astype(jnp.bfloat16)
        v = v - part.astype(jnp.float32)
        parts.append(part)
    return parts


def y_kernel(
    spread_ref, y_ref, mix_ref, other_ref, warm_ref, acc_in, acc_ref, pad_ref, mixpad_ref, flux_ref
):
    species = y_ref.shape[0]
    del acc_in
    cells = 32

    def body(x, carry):
        base = pl.multiple_of(x * cells, cells)
        own = pl.ds(base, cells)
        for side, at in ((0, 0), (8, cells + 8)):
            rows = pl.ds(pl.multiple_of(x * 16 + side, 8), 8)
            heat = warm_ref[1, rows, :]
            heat = heat * jnp.sqrt(heat)
            shares = [other_ref[j, rows, :] for j in range(species - 1)] + [warm_ref[0, rows, :]]
            for k in range(species):
                pad_ref[k, at : at + 8, :] = shares[k]
                mixpad_ref[k, at : at + 8, :] = heat / (1.0 + weighted(spread_ref, k, shares))
        for k in range(species):
            pad_ref[k, 8 : 8 + cells, :] = y_ref[k, own, :]
            mixpad_ref[k, 8 : 8 + cells, :] = mix_ref[k, own, :]
        for k in range(species):
            slope = stencil(lambda m: pad_ref[k, 4 + m : 4 + m + cells + 8, :])
            flux_ref[k] = mixpad_ref[k, 4 : 4 + cells + 8, :] * slope
        for k in range(species):
            acc_ref[k, own, :] = acc_ref[k, own, :] + flow_step * stencil(
                lambda m: flux_ref[k, 4 + m : 4 + m + cells, :]
            )
        return carry

    lax.fori_loop(0, y_ref.shape[1] // cells, body, 0)


def z_kernel(spread_ref, low_ref, high_ref, before_ref, after_ref, acc_in, acc_ref, wide_ref, diff_ref, turn_ref):
    species = acc_ref.shape[0]
    del acc_in
    diff_ref[...] = jnp.zeros_like(diff_ref)
    turn_ref[...] = jnp.zeros_like(turn_ref)

    def fluxes(first, second, h):
        for f in range(species + 1):
            wide_ref[f, :8, :] = first[2 * f + h]
            wide_ref[f, 8:, :] = second[2 * f + h]
        heat = wide_ref[species, 4:12, :]
        heat = heat * jnp.sqrt(heat)
        shares = [wide_ref[j, 4:12, :] for j in range(species)]
        result = []
        for k in range(species):
            mix = heat / (1.0 + weighted(spread_ref, k, shares))
            result.append(mix * stencil(lambda m: wide_ref[k, 4 + m : 12 + m, :]))
        return result

    for h in range(2):
        wrapped = fluxes(high_ref, low_ref, h)
        for first, second, at, put in (
            (before_ref, low_ref, 12, 0),
            (high_ref, after_ref, 4, 128 - EDGE),
        ):
            true = fluxes(first, second, h)
            for k in range(species):
                diff_ref[k, 8:16, :] = true[k] - wrapped[k]
            for k in range(species):
                turn_ref[k, put : put + 8, :] = flow_step * stencil(
                    lambda m: diff_ref[k, at + m : at + m + 8, :]
                )
        for k in range(species):
            rows = slice(h * 128, (h + 1) * 128)
            acc_ref[k, rows, :] = acc_ref[k, rows, :] + turn_ref[k].T


def inner(flux):
    cells = len(flux)
    result = []
    for x in range(cells):
        total = None
        for m in range(1, 5):
            term = None
            if x + m < cells:
                term = flux[x + m]
            if x - m >= 0:
                term = -flux[x - m] if term is None else term - flux[x - m]
            if term is not None:
                term = coefficients[m - 1] * term
                total = term if total is None else total + term
        result.append(total)
    return result


def first_kernel(y_ref, mix_ref, acc_in, before_ref, after_ref, low_ref, high_ref, acc_ref):
    del acc_in
    cells = 8

    def body(i, carry):
        k, tile = i // (FIRST // 8), i % (FIRST // 8)

        def rows(x, size=32):
            return pl.ds(pl.multiple_of(x * size + tile * 8, 8), 8)

        line = (
            [before_ref[k, rows(x), :] for x in range(4)]
            + [y_ref[k, rows(x), :] for x in range(cells)]
            + [after_ref[k, rows(x), :] for x in range(4)]
        )
        flux = [mix_ref[k, rows(x), :] * stencil(lambda m: line[x + 4 + m]) for x in range(cells)]
        for x in range(4):
            low_ref[k, rows(x, FIRST), :] = flux[x]
            high_ref[k, rows(x, FIRST), :] = flux[x + 4]
        for x, total in enumerate(inner(flux)):
            acc_ref[k, rows(x), :] = acc_ref[k, rows(x), :] + flow_step * total
        return carry

    lax.fori_loop(0, y_ref.shape[0] * (FIRST // 8), body, 0)


def second_kernel(
    spread_ref, y_ref, mix_ref, acc_in, before_ref, after_ref, left_ref, right_ref,
    acc_ref, out_ref, far_ref, sems,
):
    del acc_in
    species = y_ref.shape[0]
    cells, tiles = 8, LAST // 8

    def far(ref, k, x, tile):
        return ref[pl.ds(pl.multiple_of((k * 4 + x) * LAST + tile * 8, 8), 8), :]

    def rows(x, tile):
        return pl.ds(pl.multiple_of(x * 32 + FIRST + tile * 8, 8), 8)

    def mixing(tile, carry):
        for near_ref, ref, put in ((before_ref, left_ref, 0), (after_ref, right_ref, 4)):
            heats = [far(ref, species, x, tile) for x in range(4)]
            heats = [heat * jnp.sqrt(heat) for heat in heats]
            shares = [[near_ref[j, rows(x, tile), :] for j in range(species)] for x in range(4)]
            for k in range(species):
                weights = [spread_ref[k, j] for j in range(species)]
                for x in range(4):
                    total = 1.0
                    for weight, share in zip(weights, shares[x]):
                        total = total + weight * share
                    far_ref[tile, k, put + x] = heats[x] / total
        return carry

    lax.fori_loop(0, tiles, mixing, 0)

    def copy(k):
        here = (k, slice(None), pl.ds(FIRST, LAST), slice(None))
        return pltpu.make_async_copy(acc_ref.at[here], out_ref.at[here], sems.at[k])

    def one(k, carry):
        for tile in range(tiles):
            line = (
                [far(left_ref, k, x, tile) for x in range(4)]
                + [before_ref[k, rows(x, tile), :] for x in range(4)]
                + [y_ref[k, rows(x, tile), :] for x in range(cells)]
                + [after_ref[k, rows(x, tile), :] for x in range(4)]
                + [far(right_ref, k, x, tile) for x in range(4)]
            )
            mix = (
                [far_ref[tile, k, x] for x in range(4)]
                + [mix_ref[k, rows(x, tile), :] for x in range(cells)]
                + [far_ref[tile, k, 4 + x] for x in range(4)]
            )
            flux = [mix[x] * stencil(lambda m: line[x + 4 + m]) for x in range(cells + 8)]
            here = slice(FIRST + tile * 8, FIRST + tile * 8 + 8)
            for x in range(cells):
                total = stencil(lambda m: flux[x + 4 + m])
                acc_ref[k, x, here, :] = acc_ref[k, x, here, :] + flow_step * total
        copy(k).start()
        return carry

    lax.fori_loop(0, species, one, 0)
    lax.fori_loop(0, species, lambda k, carry: (copy(k).wait(), carry)[1], 0)


def final_kernel(acc_ref, before_ref, after_ref, out_in, out_ref, total_ref, sems):
    del out_in
    copies = []
    for k in range(acc_ref.shape[0]):
        for x in range(8):
            total = None
            for m in range(1, 5):
                if x - m < 0:
                    far = before_ref[k, (x - m + 4) * FIRST : (x - m + 5) * FIRST, :]
                    term = -coefficients[m - 1] * far
                elif x + m >= 8:
                    far = after_ref[k, (x + m - 8) * FIRST : (x + m - 7) * FIRST, :]
                    term = coefficients[m - 1] * far
                else:
                    continue
                total = term if total is None else total + term
            total_ref[k, x] = acc_ref[k, x, :FIRST, :] + flow_step * total
        here = (k, slice(None), pl.ds(0, FIRST), slice(None))
        copy = pltpu.make_async_copy(total_ref.at[k], out_ref.at[here], sems.at[k])
        copy.start()
        copies.append(copy)
    for copy in copies:
        copy.wait()


def ring(count):
    forward = [(i, (i + 1) % count) for i in range(count)]
    return forward, [(target, source) for source, target in forward]


def shards(mass, kelvin, spreads, coupling, tiles, tally):
    species, cx, cy, cz = mass.shape
    rows = cx * cy
    whole = f32(species, rows, cz)
    y = mass.reshape(species, rows, cz)
    t = kelvin.reshape(rows, cz)
    forward_x, backward_x = ring(lax.axis_size("gx"))
    forward_y, _ = ring(lax.axis_size("gy"))
    forward_z, backward_z = ring(lax.axis_size("gz"))

    def call(kernel, name, ins, out, scratch=(), aliases=None, after=(), params=PARAMS):
        operands = [array for _, array in ins] + list(after)
        specs = [spec for spec, _ in ins] + [pl.BlockSpec(memory_space=pl.ANY)] * len(after)
        single = not isinstance(out, tuple)

        def body(*refs):
            kernel(*refs[: len(ins)], *refs[len(operands) :])

        return pl.pallas_call(
            body,
            out_shape=out,
            in_specs=specs,
            out_specs=VMEM if single else (VMEM,) * len(out),
            scratch_shapes=list(scratch),
            input_output_aliases=aliases or {},
            compiler_params=params,
            name=name,
        )(*operands)

    in_hbm = pl.BlockSpec(memory_space=pl.ANY)
    upper, lower = y[:, 4 * cy :], y[:, : 4 * cy]
    before = lax.ppermute(upper, "gx", forward_x)
    after = lax.ppermute(lower, "gx", backward_x)
    facing = call(facing_kernel, "facing", [(VMEM, y)], f32(species - 1, cx * 16, cz), after=[lower, upper])
    other = lax.ppermute(facing, "gy", forward_y)
    warm = call(warm_kernel, "warm", [(VMEM, y), (VMEM, t)], f32(2, cx * 16, cz), after=[facing])
    other_t = lax.ppermute(warm, "gy", forward_y)
    packed = f32(2 * species + 2, EDGE, 128)
    low, high = call(pack_kernel, "pack", [(VMEM, y), (VMEM, t)], (packed, packed), after=[facing])
    before_z = lax.ppermute(high, "gz", forward_z)
    mix = call(mixing_kernel, "mixing", [(SMEM, spreads), (VMEM, y), (VMEM, t)], whole, after=[low, high])
    acc = call(lane_kernel, "spanwise", [(VMEM, band_matrix(cz)), (VMEM, y), (VMEM, mix)], whole)
    far = f32((species + 1) * 4 * LAST, cz)
    right, left = call(lines_kernel, "lines", [(VMEM, y), (VMEM, t)], (far, far), after=[acc, other, other_t])
    before_b = lax.ppermute(right, "gx", forward_x)
    after_b = lax.ppermute(left, "gx", backward_x)
    wide = call(extend_kernel, "extend", [(VMEM, low)], f32(WIDE, EDGE, 128), after=[left, right, before_z])
    after_z = lax.ppermute(wide, "gz", backward_z)
    acc = call(
        y_kernel,
        "transverse",
        [(SMEM, spreads)] + [(VMEM, v) for v in (y, mix, other, other_t, acc)],
        whole,
        scratch=[
            pltpu.VMEM((species, cy + 16, cz), jnp.float32),
            pltpu.VMEM((species, cy + 16, cz), jnp.float32),
            pltpu.VMEM((species, cy + 8, cz), jnp.float32),
        ],
        aliases={5: 0},
        after=[wide],
    )
    edge = f32(species, 4 * FIRST, cz)
    low_x, high_x, acc = call(
        first_kernel,
        "streamwise",
        [(VMEM, v) for v in (y, mix, acc, before, after)],
        (edge, edge, whole),
        aliases={2: 2},
        after=[],
    )
    before_a = lax.ppermute(high_x, "gx", forward_x)
    after_a = lax.ppermute(low_x, "gx", backward_x)
    acc = call(
        chem_kernel,
        "chemistry",
        [(SMEM, coupling), (SMEM, tiles), (SMEM, tally), (VMEM, y), (VMEM, t), (VMEM, acc)],
        whole,
        scratch=[
            pltpu.VMEM((species, 8, cz), jnp.float32),
            pltpu.VMEM((8, cz), jnp.float32),
            pltpu.VMEM((species, 8, cz), jnp.float32),
            pltpu.SMEM((species, species), jnp.float32),
        ],
        aliases={5: 0},
    )
    acc = call(
        z_kernel,
        "faces",
        [(SMEM, spreads)] + [(VMEM, v) for v in (low, high, before_z, after_z, acc)],
        whole,
        scratch=[
            pltpu.VMEM((species + 1, 16, 128), jnp.float32),
            pltpu.VMEM((species, 24, 128), jnp.float32),
            pltpu.VMEM((species, 128, 128), jnp.float32),
        ],
        aliases={5: 0},
    )
    result = f32(*mass.shape)
    acc, out = pl.pallas_call(
        second_kernel,
        out_shape=(result, result),
        in_specs=[SMEM] + [VMEM] * 7,
        out_specs=(VMEM, in_hbm),
        scratch_shapes=[
            pltpu.VMEM((LAST // 8, species, 8, 8, cz), jnp.float32),
            pltpu.SemaphoreType.DMA((species,)),
        ],
        input_output_aliases={3: 0},
        compiler_params=PARAMS,
        name="neighbours",
    )(spreads, y, mix, acc.reshape(mass.shape), before, after, before_b, after_b)
    return pl.pallas_call(
        final_kernel,
        out_shape=result,
        in_specs=[VMEM] * 3 + [in_hbm],
        out_specs=in_hbm,
        scratch_shapes=[
            pltpu.VMEM((species, cx, FIRST, cz), jnp.float32),
            pltpu.SemaphoreType.DMA((species,)),
        ],
        input_output_aliases={3: 0},
        compiler_params=PARAMS,
        name="finish",
    )(acc, before_a, after_a, out)


def solution(mesh):
    in_specs = (
        P(None, "gx", "gy", "gz"),
        P("gx", "gy", "gz"),
        P(),
        P(),
        P("gx", "gy", "gz", None),
        P("gx", None),
    )
    out_specs = P(None, "gx", "gy", "gz")
    return jax.shard_map(shards, mesh=mesh, in_specs=in_specs, out_specs=out_specs, check_vma=False)
```

```python
import functools

import jax
import jax.numpy as jnp
import numpy as np
from jax import lax
from jax.experimental import pallas as pl
from jax.experimental.pallas import tpu as pltpu
from jax.sharding import PartitionSpec as P

SLOTS = 64
EDGE = 8
WIDE = 75
FIRST = 16
LAST = 16

coefficients = (0.8, -0.2, 4.0 / 105.0, -1.0 / 280.0)
flow_step = 0.1
chem_step = 0.1
gamma_ros = 1.0 + 0.5**0.5
barrier_height = 2.0

VMEM = pl.BlockSpec(memory_space=pltpu.VMEM)
SMEM = pl.BlockSpec(memory_space=pltpu.SMEM)
PARAMS = pltpu.CompilerParams(vmem_limit_bytes=24 * 1024 * 1024)


def f32(*shape):
    return jax.ShapeDtypeStruct(shape, jnp.float32)


def stencil(take):
    total = None
    for m in range(1, 5):
        term = coefficients[m - 1] * (take(m) - take(-m))
        total = term if total is None else total + term
    return total


def weighted(table, k, shares):
    total = table[k, 0] * shares[0]
    for j in range(1, len(shares)):
        total = total + table[k, j] * shares[j]
    return total


def cut_kernel(y_ref, lower_ref):
    lower_ref[...] = y_ref[:, : lower_ref.shape[1], :]


def facing_rows(put_ref, f, source):
    for x in range(8):
        for at, put in ((24, 0), (0, 8)):
            put_ref[f, x * 16 + put : x * 16 + put + 8, :] = source[x * 32 + at : x * 32 + at + 8, :]


def facing_kernel(y_ref, out_ref):
    for f in range(out_ref.shape[0]):
        facing_rows(out_ref, f, y_ref.at[f])


def warm_kernel(y_ref, t_ref, out_ref):
    facing_rows(out_ref, 0, y_ref.at[y_ref.shape[0] - 1])
    facing_rows(out_ref, 1, t_ref)


def lines_kernel(y_ref, t_ref, right_ref, left_ref):
    species = y_ref.shape[0]
    for x in range(4):
        low, high = (slice(at * 32 + FIRST, at * 32 + 32) for at in (x, x + 4))
        for k in range(species + 1):
            put = slice((k * 4 + x) * LAST, (k * 4 + x + 1) * LAST)
            if k < species:
                right_ref[put, :] = y_ref[k, low, :]
                left_ref[put, :] = y_ref[k, high, :]
            else:
                right_ref[put, :] = t_ref[high, :]
                left_ref[put, :] = t_ref[low, :]


def pack_kernel(y_ref, t_ref, low_ref, high_ref):
    species = y_ref.shape[0]
    for f in range(species + 1):
        for h in range(2):
            rows = slice(h * 128, (h + 1) * 128)
            block = y_ref[f, rows, :] if f < species else t_ref[rows, :]
            turned = block.T
            low_ref[2 * f + h] = turned[:EDGE]
            high_ref[2 * f + h] = turned[128 - EDGE :]


def extend_kernel(low_ref, wide_ref):
    used = low_ref.shape[0]
    wide_ref[:used] = low_ref[...]
    wide_ref[used:] = jnp.zeros((WIDE - used, EDGE, 128), jnp.float32)


def chemistry(shares, heat, rates):
    n = len(shares)
    speed = jnp.exp(barrier_height * (1.0 - 1.0 / heat))
    scaled = (gamma_ros * chem_step) * speed

    def production(state):
        squares = [s * s for s in state]
        return [speed * weighted(rates, i, squares) for i in range(n)]

    doubled = [2.0 * (scaled * s) for s in shares]
    factors = [
        [(1.0 if i == j else 0.0) - rates[i, j] * doubled[j] for j in range(n)] for i in range(n)
    ]
    inverse = [None] * n
    for p in range(n):
        inverse[p] = 1.0 / factors[p][p]
        for r in range(p + 1, n):
            multiplier = factors[r][p] * inverse[p]
            factors[r][p] = multiplier
            for c in range(p + 1, n):
                factors[r][c] = factors[r][c] - multiplier * factors[p][c]

    def substitute(source):
        unknown = list(source)
        for r in range(n):
            for c in range(r):
                unknown[r] = unknown[r] - factors[r][c] * unknown[c]
        for r in reversed(range(n)):
            for c in range(r + 1, n):
                unknown[r] = unknown[r] - factors[r][c] * unknown[c]
            unknown[r] = unknown[r] * inverse[r]
        return unknown

    one = substitute(production(shares))
    later = production([s + chem_step * o for s, o in zip(shares, one)])
    two = substitute([g - 2.0 * o for g, o in zip(later, one)])
    return [chem_step * (1.5 * a + 0.5 * b) for a, b in zip(one, two)]


def mixing_kernel(spread_ref, y_ref, t_ref, mix_ref):
    species = y_ref.shape[0]
    step = 32

    def body(i, carry):
        rows = pl.ds(pl.multiple_of(i * step, step), step)
        heat = t_ref[rows, :]
        heat = heat * jnp.sqrt(heat)
        shares = [y_ref[j, rows, :] for j in range(species)]
        for k in range(species):
            mix_ref[k, rows, :] = heat / (1.0 + weighted(spread_ref, k, shares))
        return carry

    lax.fori_loop(0, y_ref.shape[1] // step, body, 0)


def split(v):
    parts = []
    for _ in range(3):
        part = v.astype(jnp.bfloat16)
        v = v - part.astype(jnp.float32)
        parts.append(part)
    return parts


def lane_kernel(band_ref, y_ref, mix_ref, acc_ref):

    def derivative(v):
        total = None
        for part in split(v):
            term = jnp.dot(part, band_ref[...], preferred_element_type=jnp.float32)
            total = term if total is None else total + term
        return total

    for k in range(y_ref.shape[0]):
        flux = mix_ref[k] * (derivative(y_ref[k]) * (1.0 / 840.0))
        acc_ref[k] = (flow_step / 840.0) * derivative(flux)


def band_matrix(cells):
    band = np.zeros((cells, cells), np.float32)
    for m, weight in zip(range(1, 5), (672, -168, 32, -3)):
        for i in range(cells):
            band[(i + m) % cells, i] += weight
            band[(i - m) % cells, i] -= weight
    return jnp.asarray(band, jnp.bfloat16)


def chem_kernel(
    rate_ref, tile_ref, tally_ref, y_ref, t_ref, acc_in, acc_ref, shares_ref, heat_ref, change_ref, table_ref
):
    species = y_ref.shape[0]
    del acc_in
    member = lax.axis_index("gy") * lax.axis_size("gz") + lax.axis_index("gz")
    count = tally_ref[0, member]
    for j in range(species):
        consumed = None
        for i in range(species):
            if i != j:
                consumed = rate_ref[i, j] if consumed is None else consumed + rate_ref[i, j]
        for i in range(species):
            table_ref[i, j] = -(1.25 * consumed + rate_ref[j, j]) if i == j else rate_ref[i, j]

    def body(g, carry):
        for s in range(8):
            tile = tile_ref[0, 0, 0, g * 8 + s]
            for k in range(species):
                shares_ref[k, pl.ds(s, 1), :] = y_ref[k, pl.ds(tile, 1), :]
            heat_ref[pl.ds(s, 1), :] = t_ref[pl.ds(tile, 1), :]
        change = chemistry([shares_ref[k] for k in range(species)], heat_ref[...], table_ref)
        live = g * 8 + lax.broadcasted_iota(jnp.int32, heat_ref.shape, 0) < count
        for k in range(species):
            change_ref[k] = jnp.where(live, change[k], 0.0)
        for s in range(8):
            row = pl.ds(tile_ref[0, 0, 0, g * 8 + s], 1)
            rows = [acc_ref[k, row, :] + change_ref[k, pl.ds(s, 1), :] for k in range(species)]
            for k in range(species):
                acc_ref[k, row, :] = rows[k]
        return carry

    lax.fori_loop(0, (count + 7) // 8, body, 0)


def split(v):
    parts = []
    for _ in range(3):
        part = v.astype(jnp.bfloat16)
        v = v - part.astype(jnp.float32)
        parts.append(part)
    return parts


def y_kernel(
    spread_ref, y_ref, mix_ref, other_ref, warm_ref, acc_in, acc_ref, pad_ref, mixpad_ref, flux_ref
):
    species = y_ref.shape[0]
    del acc_in
    cells = 32

    def body(x, carry):
        base = pl.multiple_of(x * cells, cells)
        own = pl.ds(base, cells)
        for side, at in ((0, 0), (8, cells + 8)):
            rows = pl.ds(pl.multiple_of(x * 16 + side, 8), 8)
            heat = warm_ref[1, rows, :]
            heat = heat * jnp.sqrt(heat)
            shares = [other_ref[j, rows, :] for j in range(species - 1)] + [warm_ref[0, rows, :]]
            for k in range(species):
                pad_ref[k, at : at + 8, :] = shares[k]
                mixpad_ref[k, at : at + 8, :] = heat / (1.0 + weighted(spread_ref, k, shares))
        for k in range(species):
            pad_ref[k, 8 : 8 + cells, :] = y_ref[k, own, :]
            mixpad_ref[k, 8 : 8 + cells, :] = mix_ref[k, own, :]
        for k in range(species):
            slope = stencil(lambda m: pad_ref[k, 4 + m : 4 + m + cells + 8, :])
            flux_ref[k] = mixpad_ref[k, 4 : 4 + cells + 8, :] * slope
        for k in range(species):
            acc_ref[k, own, :] = acc_ref[k, own, :] + flow_step * stencil(
                lambda m: flux_ref[k, 4 + m : 4 + m + cells, :]
            )
        return carry

    lax.fori_loop(0, y_ref.shape[1] // cells, body, 0)


def z_kernel(spread_ref, low_ref, high_ref, before_ref, after_ref, acc_in, acc_ref, wide_ref, diff_ref, turn_ref):
    species = acc_ref.shape[0]
    del acc_in
    diff_ref[...] = jnp.zeros_like(diff_ref)
    turn_ref[...] = jnp.zeros_like(turn_ref)

    def fluxes(first, second, h):
        for f in range(species + 1):
            wide_ref[f, :8, :] = first[2 * f + h]
            wide_ref[f, 8:, :] = second[2 * f + h]
        heat = wide_ref[species, 4:12, :]
        heat = heat * jnp.sqrt(heat)
        shares = [wide_ref[j, 4:12, :] for j in range(species)]
        result = []
        for k in range(species):
            mix = heat / (1.0 + weighted(spread_ref, k, shares))
            result.append(mix * stencil(lambda m: wide_ref[k, 4 + m : 12 + m, :]))
        return result

    for h in range(2):
        wrapped = fluxes(high_ref, low_ref, h)
        for first, second, at, put in (
            (before_ref, low_ref, 12, 0),
            (high_ref, after_ref, 4, 128 - EDGE),
        ):
            true = fluxes(first, second, h)
            for k in range(species):
                diff_ref[k, 8:16, :] = true[k] - wrapped[k]
            for k in range(species):
                turn_ref[k, put : put + 8, :] = flow_step * stencil(
                    lambda m: diff_ref[k, at + m : at + m + 8, :]
                )
        for k in range(species):
            rows = slice(h * 128, (h + 1) * 128)
            acc_ref[k, rows, :] = acc_ref[k, rows, :] + turn_ref[k].T


def inner(flux):
    cells = len(flux)
    result = []
    for x in range(cells):
        total = None
        for m in range(1, 5):
            term = None
            if x + m < cells:
                term = flux[x + m]
            if x - m >= 0:
                term = -flux[x - m] if term is None else term - flux[x - m]
            if term is not None:
                term = coefficients[m - 1] * term
                total = term if total is None else total + term
        result.append(total)
    return result


def first_kernel(y_ref, mix_ref, acc_in, before_ref, after_ref, low_ref, high_ref, acc_ref):
    del acc_in
    cells = 8

    def body(i, carry):
        k, tile = i // (FIRST // 8), i % (FIRST // 8)

        def rows(x, size=32):
            return pl.ds(pl.multiple_of(x * size + tile * 8, 8), 8)

        line = (
            [before_ref[k, rows(x), :] for x in range(4)]
            + [y_ref[k, rows(x), :] for x in range(cells)]
            + [after_ref[k, rows(x), :] for x in range(4)]
        )
        flux = [mix_ref[k, rows(x), :] * stencil(lambda m: line[x + 4 + m]) for x in range(cells)]
        for x in range(4):
            low_ref[k, rows(x, FIRST), :] = flux[x]
            high_ref[k, rows(x, FIRST), :] = flux[x + 4]
        for x, total in enumerate(inner(flux)):
            acc_ref[k, rows(x), :] = acc_ref[k, rows(x), :] + flow_step * total
        return carry

    lax.fori_loop(0, y_ref.shape[0] * (FIRST // 8), body, 0)


def second_kernel(
    spread_ref, y_ref, mix_ref, acc_in, before_ref, after_ref, left_ref, right_ref,
    acc_ref, out_ref, far_ref, sems,
):
    del acc_in
    species = y_ref.shape[0]
    cells, tiles = 8, LAST // 8

    def far(ref, k, x, tile):
        return ref[pl.ds(pl.multiple_of((k * 4 + x) * LAST + tile * 8, 8), 8), :]

    def rows(x, tile):
        return pl.ds(pl.multiple_of(x * 32 + FIRST + tile * 8, 8), 8)

    def mixing(tile, carry):
        for near_ref, ref, put in ((before_ref, left_ref, 0), (after_ref, right_ref, 4)):
            heats = [far(ref, species, x, tile) for x in range(4)]
            heats = [heat * jnp.sqrt(heat) for heat in heats]
            shares = [[near_ref[j, rows(x, tile), :] for j in range(species)] for x in range(4)]
            for k in range(species):
                weights = [spread_ref[k, j] for j in range(species)]
                for x in range(4):
                    total = 1.0
                    for weight, share in zip(weights, shares[x]):
                        total = total + weight * share
                    far_ref[tile, k, put + x] = heats[x] / total
        return carry

    lax.fori_loop(0, tiles, mixing, 0)

    def copy(k):
        here = (k, slice(None), pl.ds(FIRST, LAST), slice(None))
        return pltpu.make_async_copy(acc_ref.at[here], out_ref.at[here], sems.at[k])

    def one(k, carry):
        for tile in range(tiles):
            line = (
                [far(left_ref, k, x, tile) for x in range(4)]
                + [before_ref[k, rows(x, tile), :] for x in range(4)]
                + [y_ref[k, rows(x, tile), :] for x in range(cells)]
                + [after_ref[k, rows(x, tile), :] for x in range(4)]
                + [far(right_ref, k, x, tile) for x in range(4)]
            )
            mix = (
                [far_ref[tile, k, x] for x in range(4)]
                + [mix_ref[k, rows(x, tile), :] for x in range(cells)]
                + [far_ref[tile, k, 4 + x] for x in range(4)]
            )
            flux = [mix[x] * stencil(lambda m: line[x + 4 + m]) for x in range(cells + 8)]
            here = slice(FIRST + tile * 8, FIRST + tile * 8 + 8)
            for x in range(cells):
                total = stencil(lambda m: flux[x + 4 + m])
                acc_ref[k, x, here, :] = acc_ref[k, x, here, :] + flow_step * total
        copy(k).start()
        return carry

    lax.fori_loop(0, species, one, 0)
    lax.fori_loop(0, species, lambda k, carry: (copy(k).wait(), carry)[1], 0)


def final_kernel(acc_ref, before_ref, after_ref, out_in, out_ref, total_ref, sems):
    del out_in
    copies = []
    for k in range(acc_ref.shape[0]):
        for x in range(8):
            total = None
            for m in range(1, 5):
                if x - m < 0:
                    far = before_ref[k, (x - m + 4) * FIRST : (x - m + 5) * FIRST, :]
                    term = -coefficients[m - 1] * far
                elif x + m >= 8:
                    far = after_ref[k, (x + m - 8) * FIRST : (x + m - 7) * FIRST, :]
                    term = coefficients[m - 1] * far
                else:
                    continue
                total = term if total is None else total + term
            total_ref[k, x] = acc_ref[k, x, :FIRST, :] + flow_step * total
        here = (k, slice(None), pl.ds(0, FIRST), slice(None))
        copy = pltpu.make_async_copy(total_ref.at[k], out_ref.at[here], sems.at[k])
        copy.start()
        copies.append(copy)
    for copy in copies:
        copy.wait()


def ring(count):
    forward = [(i, (i + 1) % count) for i in range(count)]
    return forward, [(target, source) for source, target in forward]


def shards(mass, kelvin, spreads, coupling, tiles, tally):
    species, cx, cy, cz = mass.shape
    rows = cx * cy
    whole = f32(species, rows, cz)
    y = mass.reshape(species, rows, cz)
    t = kelvin.reshape(rows, cz)
    forward_x, backward_x = ring(lax.axis_size("gx"))
    forward_y, _ = ring(lax.axis_size("gy"))
    forward_z, backward_z = ring(lax.axis_size("gz"))

    def call(kernel, name, ins, out, scratch=(), aliases=None, after=(), params=PARAMS):
        operands = [array for _, array in ins] + list(after)
        specs = [spec for spec, _ in ins] + [pl.BlockSpec(memory_space=pl.ANY)] * len(after)
        single = not isinstance(out, tuple)

        def body(*refs):
            kernel(*refs[: len(ins)], *refs[len(operands) :])

        return pl.pallas_call(
            body,
            out_shape=out,
            in_specs=specs,
            out_specs=VMEM if single else (VMEM,) * len(out),
            scratch_shapes=list(scratch),
            input_output_aliases=aliases or {},
            compiler_params=params,
            name=name,
        )(*operands)

    in_hbm = pl.BlockSpec(memory_space=pl.ANY)
    upper = y[:, 4 * cy :]
    lower = call(cut_kernel, "cut", [(VMEM, y)], f32(species, 4 * cy, cz))
    before = lax.ppermute(upper, "gx", forward_x)
    after = lax.ppermute(lower, "gx", backward_x)
    facing = call(facing_kernel, "facing", [(VMEM, y)], f32(species - 1, cx * 16, cz), after=[lower])
    other = lax.ppermute(facing, "gy", forward_y)
    warm = call(warm_kernel, "warm", [(VMEM, y), (VMEM, t)], f32(2, cx * 16, cz), after=[facing])
    other_t = lax.ppermute(warm, "gy", forward_y)
    packed = f32(2 * species + 2, EDGE, 128)
    low, high = call(pack_kernel, "pack", [(VMEM, y), (VMEM, t)], (packed, packed), after=[facing])
    before_z = lax.ppermute(high, "gz", forward_z)
    mix = call(mixing_kernel, "mixing", [(SMEM, spreads), (VMEM, y), (VMEM, t)], whole, after=[low, high])
    acc = call(lane_kernel, "spanwise", [(VMEM, band_matrix(cz)), (VMEM, y), (VMEM, mix)], whole)
    far = f32((species + 1) * 4 * LAST, cz)
    right, left = call(lines_kernel, "lines", [(VMEM, y), (VMEM, t)], (far, far), after=[acc, other, other_t])
    before_b = lax.ppermute(right, "gx", forward_x)
    after_b = lax.ppermute(left, "gx", backward_x)
    wide = call(extend_kernel, "extend", [(VMEM, low)], f32(WIDE, EDGE, 128), after=[left, right, before_z])
    after_z = lax.ppermute(wide, "gz", backward_z)
    acc = call(
        y_kernel,
        "transverse",
        [(SMEM, spreads)] + [(VMEM, v) for v in (y, mix, other, other_t, acc)],
        whole,
        scratch=[
            pltpu.VMEM((species, cy + 16, cz), jnp.float32),
            pltpu.VMEM((species, cy + 16, cz), jnp.float32),
            pltpu.VMEM((species, cy + 8, cz), jnp.float32),
        ],
        aliases={5: 0},
        after=[wide],
    )
    edge = f32(species, 4 * FIRST, cz)
    low_x, high_x, acc = call(
        first_kernel,
        "streamwise",
        [(VMEM, v) for v in (y, mix, acc, before, after)],
        (edge, edge, whole),
        aliases={2: 2},
        after=[],
    )
    before_a = lax.ppermute(high_x, "gx", forward_x)
    after_a = lax.ppermute(low_x, "gx", backward_x)
    acc = call(
        chem_kernel,
        "chemistry",
        [(SMEM, coupling), (SMEM, tiles), (SMEM, tally), (VMEM, y), (VMEM, t), (VMEM, acc)],
        whole,
        scratch=[
            pltpu.VMEM((species, 8, cz), jnp.float32),
            pltpu.VMEM((8, cz), jnp.float32),
            pltpu.VMEM((species, 8, cz), jnp.float32),
            pltpu.SMEM((species, species), jnp.float32),
        ],
        aliases={5: 0},
    )
    acc = call(
        z_kernel,
        "faces",
        [(SMEM, spreads)] + [(VMEM, v) for v in (low, high, before_z, after_z, acc)],
        whole,
        scratch=[
            pltpu.VMEM((species + 1, 16, 128), jnp.float32),
            pltpu.VMEM((species, 24, 128), jnp.float32),
            pltpu.VMEM((species, 128, 128), jnp.float32),
        ],
        aliases={5: 0},
    )
    result = f32(*mass.shape)
    acc, out = pl.pallas_call(
        second_kernel,
        out_shape=(result, result),
        in_specs=[SMEM] + [VMEM] * 7,
        out_specs=(VMEM, in_hbm),
        scratch_shapes=[
            pltpu.VMEM((LAST // 8, species, 8, 8, cz), jnp.float32),
            pltpu.SemaphoreType.DMA((species,)),
        ],
        input_output_aliases={3: 0},
        compiler_params=PARAMS,
        name="neighbours",
    )(spreads, y, mix, acc.reshape(mass.shape), before, after, before_b, after_b)
    return pl.pallas_call(
        final_kernel,
        out_shape=result,
        in_specs=[VMEM] * 3 + [in_hbm],
        out_specs=in_hbm,
        scratch_shapes=[
            pltpu.VMEM((species, cx, FIRST, cz), jnp.float32),
            pltpu.SemaphoreType.DMA((species,)),
        ],
        input_output_aliases={3: 0},
        compiler_params=PARAMS,
        name="finish",
    )(acc, before_a, after_a, out)


def solution(mesh):
    in_specs = (
        P(None, "gx", "gy", "gz"),
        P("gx", "gy", "gz"),
        P(),
        P(),
        P("gx", "gy", "gz", None),
        P("gx", None),
    )
    out_specs = P(None, "gx", "gy", "gz")
    return jax.shard_map(shards, mesh=mesh, in_specs=in_specs, out_specs=out_specs, check_vma=False)
```
